32 devices in a mesh: batch: 8 (over z, y), mp: 4 (over x, core).
Axes of the slice: x: 2, y: 2, z: 4, core: 2. Of those that a mesh axis runs over, the one named last changes fastest.
Arguments:
- img_feat: bfloat16 [16384, 768], P(('batch', 'mp')), may hold values from -6 to 6
- txt_feat: bfloat16 [16384, 768], P(('batch', 'mp')), may hold values from -6 to 6
- img_proj: bfloat16 [768, 768], P('mp'), may hold values from -0.21875 to 0.21875
- txt_proj: bfloat16 [768, 768], P('mp'), may hold values from -0.21875 to 0.21875
- logit_scale: float32 [], replicated, may hold values from 2 to 3
- bias: float32 [], replicated, may hold values from -2 to 0
Outputs:
- mean_loss: float32 [], replicated
- grad_logit_scale: float32 [], replicated
- grad_bias: float32 [], replicated
- grad_img_proj: float32 [768, 768], P('mp')
- grad_txt_proj: float32 [768, 768], P('mp')
The draws below stay inside these ranges and needn't reach their ends.
All inputs are finite; a program needn't handle non-finite values.
Results may differ from the reference program's by a relative error of at most 0.0008.
Values may be sent and summed in bfloat16 or wider, within the bound.
No kernel may reach another device: no remote copies, remote signals or barrier semaphores. Data moves between devices by JAX's collectives and lax.ppermute only.
A program may use at most 128 MiB of HBM per device.

```python
import jax
import jax.numpy as jnp
from jax import lax

E = 768
D = 768
ROWS = 512
GROUP = 8
IMAGES = 16384
N_BATCH = 8
N_MP = 4


def levels(stream_key, extent, pieces, least, high):
    factor_of, own = 1.0, jax.random.fold_in(stream_key, 6)
    for position, parts in pieces:
        heights = jnp.exp(jax.random.uniform(jax.random.fold_in(own, position), (parts,), jnp.float32, least / len(pieces), high / len(pieces)))
        factor_of = factor_of * jnp.repeat(heights, extent[position] // parts).reshape([-1 if axis == position else 1 for axis in range(len(extent))])
    return factor_of


def normal_values(own_key, dims, deviation, most, pieces=(), dtype=jnp.bfloat16):
    entries = deviation * jax.random.normal(own_key, dims, jnp.float32)
    if pieces:
        entries = entries * levels(own_key, dims, pieces, -0.22, 0.18)
    return jnp.clip(entries, -most, most).astype(dtype)


def setup_inputs(seed: int = 0) -> dict:
    keys = jax.random.split(jax.random.key(seed), 7)
    img_feat = normal_values(keys[0], (IMAGES, E), 1.0, 6.0, ((0, 32),))
    txt_feat = normal_values(keys[1], (IMAGES, E), 1.0, 6.0, ((0, 32),))
    img_proj = normal_values(keys[2], (E, D), E ** -0.5, 0.21875, ((0, 4),))
    txt_proj = normal_values(keys[3], (E, D), E ** -0.5, 0.21875, ((0, 4),))
    logit_scale = jnp.clip(jax.random.uniform(keys[4], (), jnp.float32, 2.0, 3.0), 2.0, 3.0)
    bias = jnp.clip(jax.random.uniform(keys[5], (), jnp.float32, -2.0, 0.0), -2.0, 0.0)
    return {"img_feat": img_feat, "txt_feat": txt_feat, "img_proj": img_proj, "txt_proj": txt_proj, "logit_scale": logit_scale, "bias": bias}


def normalize(u):
    r = lax.rsqrt(lax.optimization_barrier(jnp.sum(u * u, axis=1, keepdims=True)) + 1e-06)
    zf = u * r
    return (zf, r, zf.astype(jnp.bfloat16))

def regroup(z):
    z = z.reshape(N_BATCH // GROUP, GROUP, N_MP, ROWS, z.shape[-1])
    z = jnp.transpose(z, (0, 2, 1, 3, 4))
    return z.reshape(N_BATCH // GROUP * N_MP, GROUP * ROWS, z.shape[-1])

def ungroup(z):
    z = z.reshape(N_BATCH // GROUP, N_MP, GROUP, ROWS, z.shape[-1])
    z = jnp.transpose(z, (0, 2, 1, 3, 4))
    return z.reshape(IMAGES, z.shape[-1])

def reference(img_feat, txt_feat, img_proj, txt_proj, logit_scale, bias):
    u_img = jnp.dot(img_feat, img_proj, preferred_element_type=jnp.float32)
    u_txt = jnp.dot(txt_feat, txt_proj, preferred_element_type=jnp.float32)
    zf_img, r_img, z_img = normalize(u_img)
    zf_txt, r_txt, z_txt = normalize(u_txt)
    scale = jnp.exp(logit_scale)
    width = GROUP * ROWS
    index = jnp.arange(width)
    sign = jnp.where(index[:, None] == index[None, :], 1.0, -1.0).astype(jnp.float32)

    def one_group(pair):
        left, right = pair
        sims = jnp.dot(left, right.T, preferred_element_type=jnp.float32)
        logit = scale * sims + bias
        loss = jnp.sum(jax.nn.softplus(-sign * logit)) / width
        grads = -sign * jax.nn.sigmoid(-sign * logit) / width
        gsum = jnp.sum(grads)
        gscale = jnp.sum(grads * scale * sims)
        gb = grads.astype(jnp.bfloat16)
        dz_img = scale * jnp.dot(gb, right, preferred_element_type=jnp.float32)
        dz_txt = scale * jnp.dot(gb.T, left, preferred_element_type=jnp.float32)
        return (dz_img, dz_txt, loss, gsum, gscale)
    dz_img, dz_txt, losses, gsums, gscales = lax.map(one_group, (regroup(z_img), regroup(z_txt)))
    dz_img = ungroup(dz_img)
    dz_txt = ungroup(dz_txt)

    def back(dz, zf, r):
        return (r * (dz - zf * lax.optimization_barrier(jnp.sum(zf * dz, axis=1, keepdims=True)))).astype(jnp.bfloat16)
    du_img = back(dz_img, zf_img, r_img)
    du_txt = back(dz_txt, zf_txt, r_txt)
    grad_img = jnp.dot(img_feat.T, du_img, preferred_element_type=jnp.float32)
    grad_txt = jnp.dot(txt_feat.T, du_txt, preferred_element_type=jnp.float32)
    mean_loss = jnp.sum(losses) / IMAGES
    grad_scale = jnp.sum(gscales) / IMAGES
    grad_bias = jnp.sum(gsums) / IMAGES
    return (mean_loss, grad_scale, grad_bias, grad_img, grad_txt)
```

```python
import functools

import jax
import jax.numpy as jnp
from jax import lax
from jax.experimental import pallas as pl
from jax.experimental.pallas import tpu as pltpu
from jax.sharding import PartitionSpec as P

AXES = ("batch", "mp")
LOG2E = 1.4426950408889634
TILE = 512
F32 = jnp.float32
BF16 = jnp.bfloat16


def bits(i):
    b, m = divmod(i, 4)
    return b & 1, b >> 1 & 1, b >> 2 & 1, m & 1


def is_home(i):
    y, zl, zh, c = bits(i)
    return c == zh


def pairs(n, flip, keep=None):
    return [(i, i ^ flip) for i in range(n) if keep is None or keep(i)]


C, X, Y, ZL, ZH = 1, 2, 4, 8, 16


def project(feat, w):
    u = jnp.dot(feat, w, preferred_element_type=F32)
    r = lax.rsqrt(jnp.sum(u * u, axis=1, keepdims=True) + 1e-06)
    return u * r, r


def pair_kernel(rows, width, flags, scal, *refs):
    home_m, rem_m = refs[0:2], refs[2:4]
    h_own, h_sib = refs[4:8], refs[8:12]
    r_own, r_sib = refs[12:16], refs[16:20]
    wparts = refs[20:24]
    g_out, stats = refs[24:26]
    w_m, w_o, feat, z_m, zf_m, r_m, z_o, acc, grad, logs, sums, prods = refs[26:]
    home, m, y = flags[0], flags[1], flags[2]
    scale, bias = scal[0], scal[1]
    part = wparts[0].shape[0] // 2
    is_h = home == 1

    for j in range(4):
        at = pl.multiple_of((m ^ j) * part, part)
        w_m[pl.ds(at, part), :] = wparts[j][:part, :]
        w_o[pl.ds(at, part), :] = wparts[j][part:, :]

    def own(i, ref):
        feat[i * rows:(i + 1) * rows, :] = ref[...]

    @pl.when(is_h)
    def _():
        for i in range(2):
            own(i, home_m[i])

    @pl.when(jnp.logical_not(is_h))
    def _():
        for i in range(2):
            own(i, rem_m[i])

    for i in range(2):
        zf, r = project(feat[i * rows:(i + 1) * rows, :], w_m[...])
        zf_m[i * rows:(i + 1) * rows, :] = zf
        r_m[i * rows:(i + 1) * rows, :] = r
        z_m[i * rows:(i + 1) * rows, :] = zf.astype(BF16)

    def other(k, ref):
        zf, r = project(ref[...], w_o[...])
        z_o[k * rows:(k + 1) * rows, :] = zf.astype(BF16)

    @pl.when(is_h)
    def _():
        for k in range(4):
            other(k, h_own[k])
            other(4 + k, r_sib[k])

    @pl.when(jnp.logical_not(is_h))
    def _():
        for k in range(4):
            other(k, r_own[k])
            other(4 + k, h_sib[k])

    acc[...] = jnp.zeros_like(acc)
    logs[...] = jnp.zeros_like(logs)
    sums[...] = jnp.zeros_like(sums)
    prods[...] = jnp.zeros_like(prods)
    a = scale * LOG2E
    b = bias * LOG2E
    step = 256
    n_i = 2 * rows // step

    def fold(v):
        return jnp.sum(v.reshape(v.shape[0] // 8, 8, v.shape[1]), axis=0)

    def sims(i, zo):
        return lax.dot_general(z_m[i * step:(i + 1) * step, :], zo, (((1,), (1,)), ((), ())), preferred_element_type=F32)

    def body(j, _):
        zo = z_o[pl.ds(pl.multiple_of(j * TILE, TILE), TILE), :]
        s = sims(0, zo)
        for i in range(n_i):
            ahead = sims(i + 1, zo) if i + 1 < n_i else None
            t = jnp.exp2(s * a + b)
            d = 1.0 + t
            sig = t * pl.reciprocal(d, approx=False)
            q = step // 4
            d4 = (d[:q] * d[q:2 * q]) * (d[2 * q:3 * q] * d[3 * q:])
            logs[...] += fold(jnp.log(d4))
            sums[...] += fold(sig)
            prods[...] += fold(sig * s)
            acc[i * step:(i + 1) * step, :] += jnp.dot(sig.astype(BF16), zo, preferred_element_type=F32)
            s = ahead
        return 0

    lax.fori_loop(0, width // TILE, body, 0)

    zo = z_o[:2 * rows, :].astype(F32)
    s_own = jnp.sum(z_m[...].astype(F32) * zo, axis=1, keepdims=True)
    l_own = scale * s_own + bias
    t = jnp.exp2(s_own * a + b)
    sig = t * pl.reciprocal(1.0 + t, approx=False)
    g_neg = sig.astype(BF16).astype(F32)
    g_own = (-pl.reciprocal(1.0 + t, approx=False)).astype(BF16).astype(F32)
    dz = (scale / width) * (acc[...] + (g_own - g_neg) * zo)
    zf = zf_m[...]
    du = (r_m[...] * (dz - zf * jnp.sum(zf * dz, axis=1, keepdims=True))).astype(BF16)
    grad[...] = lax.dot_general(feat[...], du, (((0,), (0,)), ((), ())), preferred_element_type=F32)
    half = part // 2
    for j in range(4):
        for h in range(2):
            at = pl.multiple_of((m ^ j) * part + (y ^ h) * half, half)
            k = 2 * j + h
            g_out[k * half:(k + 1) * half, :] = grad[pl.ds(at, half), :]
    loss = (jnp.sum(logs[...]) - jnp.sum(l_own)) / width
    gsum = (jnp.sum(sums[...]) - 2 * rows) / width
    gscale = scale * (jnp.sum(prods[...]) - jnp.sum(s_own)) / width
    row = lax.broadcasted_iota(jnp.int32, stats.shape, 0)
    stats[...] = jnp.where(row == 0, loss, jnp.where(row == 1, gsum, jnp.where(row == 2, gscale, 0.0)))


def per_device(n_batch, img_feat, txt_feat, img_proj, txt_proj, logit_scale, bias):
    rows, width_in = img_feat.shape
    embed = img_proj.shape[1]
    n = n_batch * 4
    width = 8 * rows
    b = lax.axis_index("batch")
    m = lax.axis_index("mp")
    y, zl, zh, c = b & 1, b >> 1 & 1, b >> 2 & 1, m & 1
    home = (c == zh).astype(jnp.int32)
    images = zl == 0

    def send(v, flip, keep=None):
        return lax.ppermute(v, AXES, pairs(n, flip, keep))

    def away(i):
        return not is_home(i)

    opp = jnp.where(images, txt_feat, img_feat)
    mine = jnp.where(images, img_feat, txt_feat)
    swap_o = send(opp, ZH | C, away)
    swap_m = send(mine, ZH | C, away)
    w0 = jnp.concatenate([jnp.where(images, img_proj, txt_proj), jnp.where(images, txt_proj, img_proj)], axis=0)
    w2 = send(w0, X)
    w1 = send(w0, C)
    w3 = send(w2, C)
    h = [opp, send(mine, ZL, is_home), send(opp, Y, is_home)]
    home_m2 = send(opp, ZL, is_home)
    h.append(send(h[1], Y, is_home))
    r = [swap_o, send(swap_m, ZL, away), send(swap_o, Y, away)]
    rem_m2 = send(swap_o, ZL, away)
    r.append(send(r[1], Y, away))
    h_sib = [send(v, C, is_home) for v in h]
    r_sib = [send(v, C, away) for v in r]

    flags = jnp.stack([home, m, y])
    scal = jnp.stack([jnp.exp(logit_scale), bias])
    smem = pl.BlockSpec(memory_space=pltpu.SMEM)
    vmem = pl.BlockSpec(memory_space=pltpu.VMEM)
    grads, stats = pl.pallas_call(
        functools.partial(pair_kernel, rows, width),
        out_shape=(
            jax.ShapeDtypeStruct((width_in, embed), F32),
            jax.ShapeDtypeStruct((8, 128), F32),
        ),
        in_specs=[smem, smem] + [vmem] * 24,
        out_specs=(vmem, vmem),
        scratch_shapes=[
            pltpu.VMEM((width_in, embed), BF16),
            pltpu.VMEM((width_in, embed), BF16),
            pltpu.VMEM((2 * rows, width_in), BF16),
            pltpu.VMEM((2 * rows, embed), BF16),
            pltpu.VMEM((2 * rows, embed), F32),
            pltpu.VMEM((2 * rows, 1), F32),
            pltpu.VMEM((width, embed), BF16),
            pltpu.VMEM((2 * rows, embed), F32),
            pltpu.VMEM((width_in, embed), F32),
            pltpu.VMEM((8, TILE), F32),
            pltpu.VMEM((8, TILE), F32),
            pltpu.VMEM((8, TILE), F32),
        ],
        compiler_params=pltpu.CompilerParams(vmem_limit_bytes=58 * 2**20),
    )(flags, scal, mine, home_m2, swap_m, rem_m2, *h, *h_sib, *r, *r_sib, w0, w1, w2, w3)

    half = width_in // 8
    g = [grads[k * half:(k + 1) * half] for k in range(8)]
    got = send(jnp.concatenate([g[2], g[3], g[6], g[7]], axis=0), C)
    own_y, own_n, x_y, x_n = (a + got[k * half:(k + 1) * half] for k, a in enumerate((g[0], g[1], g[4], g[5])))
    total = (own_y + send(x_y, X)) + (send(own_n, Y) + send(x_n, X | Y))
    total = total + send(total, ZH)
    scalars = jnp.where(images, stats, 0.0)
    for flip in (C, X, Y, ZL, ZH):
        scalars = scalars + send(scalars, flip)
    flip = 2 * ZH
    while flip < n:
        total = total + send(total, flip)
        scalars = scalars + send(scalars, flip)
        flip *= 2
    here = [total, send(total, Y)]
    there = [send(total, ZL), send(total, ZL | Y)]

    def order(v):
        return jnp.concatenate([jnp.where(y == 0, v[0], v[1]), jnp.where(y == 0, v[1], v[0])], axis=0)

    here, there = order(here), order(there)
    count = rows * n
    return (
        scalars[0, 0] / count,
        scalars[2, 0] / count,
        scalars[1, 0] / count,
        jnp.where(images, here, there),
        jnp.where(images, there, here),
    )


def solution(mesh):
    return jax.shard_map(
        functools.partial(per_device, mesh.shape["batch"]),
        mesh=mesh,
        in_specs=(
            P(AXES, None),
            P(AXES, None),
            P("mp", None),
            P("mp", None),
            P(),
            P(),
        ),
        out_specs=(P(), P(), P(), P("mp", None), P("mp", None)),
        check_vma=False,
    )
```

```python
import functools

import jax
import jax.numpy as jnp
from jax import lax
from jax.experimental import pallas as pl
from jax.experimental.pallas import tpu as pltpu
from jax.sharding import PartitionSpec as P

AXES = ("batch", "mp")
LOG2E = 1.4426950408889634
STEP = 256
F32 = jnp.float32
F16 = jnp.float16
BF16 = jnp.bfloat16
C, X, Y, ZL, ZH = 1, 2, 4, 8, 16
ANY = pl.BlockSpec(memory_space=pl.ANY)
SMEM = pl.BlockSpec(memory_space=pltpu.SMEM)
VMEM = pl.BlockSpec(memory_space=pltpu.VMEM)


def is_home(i):
    b, m = divmod(i, 4)
    return m & 1 == b >> 2 & 1


def pairs(n, home, away):
    flips = [home if is_home(i) else away for i in range(n)]
    return [(i, i ^ f) for i, f in enumerate(flips) if f is not None]


def normalize(u):
    r = lax.rsqrt(jnp.sum(u * u, axis=1, keepdims=True) + 1e-06)
    return u * r, r


def project(feat, w):
    return normalize(jnp.dot(feat, w, preferred_element_type=F32))


def fold(v):
    return jnp.sum(v.reshape(v.shape[0] // 8, 8, v.shape[1]), axis=0)


def fetch(flags, pair, dst, sem):
    if not isinstance(pair, tuple):
        copy = pltpu.make_async_copy(pair, dst, sem)
        copy.start()
        return copy
    first, second = (pltpu.make_async_copy(p, dst, sem) for p in pair)

    @pl.when(flags[0] == 1)
    def _():
        first.start()

    @pl.when(flags[0] != 1)
    def _():
        second.start()

    return first


def pair_terms(scal, z_m, lo, hi, zo, acc, stats):
    a = scal[0] * LOG2E
    b = scal[1] * LOG2E

    def sims(i):
        return lax.dot_general(z_m[i:i + STEP, :], zo, (((1,), (1,)), ((), ())), preferred_element_type=F32)

    s = sims(lo)
    for i in range(lo, hi, STEP):
        ahead = sims(i + STEP) if i + STEP < hi else None
        t = jnp.exp2(s * a + b)
        d = 1.0 + t
        sig = t * pltpu.reciprocal(d, approx=False)
        q = STEP // 4
        d4 = (d[:q] * d[q:2 * q]) * (d[2 * q:3 * q] * d[3 * q:])
        stats[0] += fold(jnp.log(d4))
        stats[1] += fold(sig)
        stats[2] += fold(sig * s)
        acc[i:i + STEP, :] += jnp.dot(sig.astype(BF16), zo, preferred_element_type=F32)
        s = ahead


def first_kernel(flags, scal, w0, w1, w2, w3, m_h, m_a, o0_h, o0_a, o1_h, o1_a,
                 w_m, w_o, z_m, zf, r_out, acc, z_o, stats, w_in, f_in, sems):
    rows = f_in.shape[0] // 3
    part = w0.shape[0] // 2
    m = flags[1]
    copies = [fetch(flags, w, w_in.at[j], sems.at[j]) for j, w in enumerate((w0, w1, w2, w3))]
    copies += [
        fetch(flags, p, f_in.at[pl.ds(k * rows, rows), :], sems.at[4 + k])
        for k, p in enumerate(((m_h, m_a), (o0_h, o0_a), (o1_h, o1_a)))
    ]
    acc[...] = jnp.zeros_like(acc)
    stats[...] = jnp.zeros_like(stats)
    for j in range(4):
        copies[j].wait()
        at = pl.multiple_of((m ^ j) * part, part)
        w_m[pl.ds(at, part), :] = w_in[j, :part, :]
        w_o[pl.ds(at, part), :] = w_in[j, part:, :]
    copies[4].wait()
    zf_m, r = project(f_in[:rows, :], w_m[...])
    zf[...] = zf_m
    r_out[...] = jnp.broadcast_to(r, r_out.shape)
    z_m[...] = zf_m.astype(BF16)
    for k in range(2):
        copies[5 + k].wait()
        z_o[k * rows:(k + 1) * rows, :] = project(f_in[(k + 1) * rows:(k + 2) * rows, :], w_o[...])[0].astype(BF16)
    pair_terms(scal, z_m, 0, rows, z_o[...], acc, stats)


def next_kernel(flags, scal, w_o, z_m, acc_in, stats_in, o0_h, o0_a, o1_h, o1_a, acc, z_o, stats, w_in, f_in, z_in, sems):
    rows = z_in.shape[0]
    copies = [fetch(flags, w_o, w_in, sems.at[0])]
    copies += [
        fetch(flags, p, f_in.at[pl.ds(k * rows, rows), :], sems.at[1 + k])
        for k, p in enumerate(((o0_h, o0_a), (o1_h, o1_a)))
    ]
    copies += [
        fetch(flags, z_m, z_in, sems.at[3]),
        fetch(flags, acc_in, acc, sems.at[4]),
        fetch(flags, stats_in, stats, sems.at[5]),
    ]
    copies[0].wait()
    for k in range(2):
        copies[1 + k].wait()
        z_o[k * rows:(k + 1) * rows, :] = project(f_in[k * rows:(k + 1) * rows, :], w_in[...])[0].astype(BF16)
    for k in range(3, 6):
        copies[k].wait()
    pair_terms(scal, z_in, 0, rows, z_o[...], acc, stats)


def last_kernel(width, flags, scal, w_m, w_o, z_m, zf_m, r_m, acc_in, stats_in, zo_a, zo_b, zo_c, m0_h, m0_a, m1_h, m1_a,
                o0_h, o0_a, o1_h, o1_a, g_out, w_in, feat, f_in, z, zf, r, z_o, acc, stats, grad, sems):
    rows = zf_m.shape[0]
    home, m, y = flags[0], flags[1], flags[2]
    scale, bias = scal[0], scal[1]

    def span(k):
        return pl.ds(k * rows, rows)

    def get(k, src, dst):
        return fetch(flags, src, dst, sems.at[k])

    c_wm = get(0, w_m, w_in.at[0])
    c_m1 = get(1, (m1_h, m1_a), feat.at[span(1), :])
    c_zo = [get(2 + k, v, z_o.at[k]) for k, v in enumerate((zo_a, zo_b, zo_c))]
    c_wo = get(5, w_o, w_in.at[1])
    c_o = [get(6 + k, p, f_in.at[span(k), :]) for k, p in enumerate(((o0_h, o0_a), (o1_h, o1_a)))]
    c_st = get(8, stats_in, stats)
    c_z = get(9, z_m, z.at[span(0), :])
    c_acc = get(10, acc_in, acc.at[span(0), :])
    c_zf = get(11, zf_m, zf.at[span(0), :])
    c_r = get(12, r_m, r)
    c_m0 = get(13, (m0_h, m0_a), feat.at[span(0), :])
    acc[rows:, :] = jnp.zeros_like(acc[rows:, :])
    c_wm.wait()
    c_m1.wait()
    zf_1, r_1 = project(feat[rows:, :], w_in[0])
    zf[rows:, :] = zf_1
    z[rows:, :] = zf_1.astype(BF16)
    c_st.wait()
    for k in range(3):
        c_zo[k].wait()
        pair_terms(scal, z, rows, 2 * rows, z_o[k], acc, stats)
    c_wo.wait()
    for k in range(2):
        c_o[k].wait()
        z_o[3, k * rows:(k + 1) * rows, :] = project(f_in[k * rows:(k + 1) * rows, :], w_in[1])[0].astype(BF16)
    c_z.wait()
    c_acc.wait()
    pair_terms(scal, z, 0, 2 * rows, z_o[3], acc, stats)
    c_zf.wait()
    c_r.wait()
    c_m0.wait()

    def finish(k, r_k, z_own):
        at = slice(k * rows, (k + 1) * rows)
        z_own = z_own.astype(F32)
        s = jnp.sum(z[at, :].astype(F32) * z_own, axis=1, keepdims=True)
        l = scale * s + bias
        t = jnp.exp2(s * (scale * LOG2E) + bias * LOG2E)
        rest = pltpu.reciprocal(1.0 + t, approx=False)
        change = (-rest).astype(BF16).astype(F32) - (t * rest).astype(BF16).astype(F32)
        dz = (scale / width) * (acc[at, :] + change * z_own)
        zf_k = zf[at, :]
        du = (r_k * (dz - zf_k * jnp.sum(zf_k * dz, axis=1, keepdims=True))).astype(BF16)
        return du, jnp.sum(s), jnp.sum(l)

    own_0 = jnp.where(home == 1, z_o[0, :rows, :], z_o[2, :rows, :])
    own_1 = jnp.where(home == 1, z_o[0, rows:, :], z_o[1, :rows, :])
    du_0, s_0, l_0 = finish(0, r[:, :1], own_0)
    du_1, s_1, l_1 = finish(1, r_1, own_1)
    grad[...] = lax.dot_general(
        feat[...], jnp.concatenate([du_0, du_1], axis=0), (((0,), (0,)), ((), ())), preferred_element_type=F32
    )
    half = grad.shape[0] // 8
    for j in range(4):
        for h in range(2):
            at = pl.multiple_of((m ^ j) * 2 * half + (y ^ h) * half, half)
            k = 2 * j + h
            g_out[k * half:(k + 1) * half, :] = grad[pl.ds(at, half), :]
    most = jnp.max(jnp.abs(grad[...]))
    loss = (jnp.sum(stats[0]) - (l_0 + l_1)) / width
    gsum = (jnp.sum(stats[1]) - 2 * rows) / width
    gscale = scale * (jnp.sum(stats[2]) - (s_0 + s_1)) / width
    tail = g_out.shape[0] - 8 * half
    row = lax.broadcasted_iota(jnp.int32, (tail, g_out.shape[1]), 0)
    values = jnp.zeros((tail, g_out.shape[1]), F32)
    for k, v in enumerate((most, loss, gsum, gscale)):
        values = jnp.where(row == k, v, values)
    g_out[8 * half:, :] = values


def call(kernel, outs, inputs, scratch, sems, flops):
    def spec(v):
        return SMEM if v.ndim == 1 else ANY

    return pl.pallas_call(
        kernel,
        out_shape=[jax.ShapeDtypeStruct(*o) for o in outs],
        in_specs=[spec(v) for v in inputs],
        out_specs=[VMEM] * len(outs),
        scratch_shapes=[pltpu.VMEM(*s) for s in scratch] + [pltpu.SemaphoreType.DMA((sems,))],
        compiler_params=pltpu.CompilerParams(vmem_limit_bytes=48 * 2**20),
        cost_estimate=pl.CostEstimate(flops=flops, bytes_accessed=8 * 2**20, transcendentals=0),
    )(*inputs)


def half_round(v):
    return lax.reduce_precision(v, exponent_bits=5, mantissa_bits=10)


def encode(values, power, scalars):
    high = half_round(scalars)
    low = half_round(scalars - high)
    row = lax.broadcasted_iota(jnp.int32, (16, values.shape[1]), 0)
    tail = jnp.where(row == 0, power, 0.0)
    for k in range(3):
        tail = jnp.where(row == 1 + k, high[k], jnp.where(row == 4 + k, low[k], tail))
    return jnp.concatenate([half_round(values * jnp.exp2(power)), tail], axis=0).astype(F16)


def decode(message):
    rows = message.shape[0] - 16
    tail = message[rows:, 0].astype(F32)
    return message[:rows].astype(F32) * jnp.exp2(-tail[0]), tail[0], tail[1:4] + tail[4:7]


def per_device(n_batch, img_feat, txt_feat, img_proj, txt_proj, logit_scale, bias):
    rows, wide = img_feat.shape
    embed = img_proj.shape[1]
    n = n_batch * 4
    width = 8 * rows
    b = lax.axis_index("batch")
    m = lax.axis_index("mp")
    y, zl, zh, c = b & 1, b >> 1 & 1, b >> 2 & 1, m & 1
    home = (c == zh).astype(jnp.int32)
    images = zl == 0
    flags = jnp.stack([home, m, y])
    scal = jnp.stack([jnp.exp(logit_scale), bias])

    def send(v, home, away):
        return lax.ppermute(v, AXES, pairs(n, home, away))

    def both(v, flip):
        return send(v, flip, flip)

    swap = ZH | C
    mine = jnp.where(images, img_feat, txt_feat)
    opp = jnp.where(images, txt_feat, img_feat)
    w0 = jnp.concatenate([jnp.where(images, img_proj, txt_proj), jnp.where(images, txt_proj, img_proj)], axis=0)
    p1 = send(mine, ZL, swap)
    w2 = both(w0, X)
    w1 = both(w0, C)
    s0 = send(opp, C, None)
    p1, w2, opp_late = lax.optimization_barrier((p1, w2, opp))
    p2 = send(opp_late, Y, swap)
    p3 = send(p1, Y, ZL)
    w3 = both(w2, C)
    s1 = send(p1, C, None)
    p7 = send(opp, ZL, None)

    wide_sq = (wide, embed)
    two = (2 * rows, embed)
    one = (rows, embed)
    stat = (3, 8, 2 * rows)
    unit = 2 * rows * rows * embed
    w_m, w_o, z_m, zf, r, acc, zo_a, stats = call(
        first_kernel,
        [(wide_sq, BF16), (wide_sq, BF16), (one, BF16), (one, F32), ((rows, 128), F32), (one, F32), (two, BF16), (stat, F32)],
        [flags, scal, w0, w1, w2, w3, mine, p1, opp, s0, p1, s1],
        [((4, *w0.shape), BF16), ((3 * rows, wide), BF16)],
        7,
        8 * unit,
    )

    def middle(z_m, acc, stats, o0_h, o0_a, o1_h, o1_a):
        return call(
            next_kernel,
            [(one, F32), (two, BF16), (stat, F32)],
            [flags, scal, w_o, z_m, acc, stats, o0_h, o0_a, o1_h, o1_a],
            [(wide_sq, BF16), ((2 * rows, wide), BF16), (one, BF16)],
            6,
            6 * unit,
        )

    p3, acc = lax.optimization_barrier((p3, acc))
    s3 = both(p3, C)
    p5 = send(p3, None, Y)
    acc, zo_b, stats = middle(z_m, acc, stats, p3, p3, s3, s3)
    p2, acc = lax.optimization_barrier((p2, acc))
    p4 = send(p2, None, Y)
    p6 = send(p2, None, ZL)
    s2 = both(p2, C)
    acc, zo_c, stats = middle(z_m, acc, stats, p2, p2, s2, s2)
    p5, p4, p6, acc = lax.optimization_barrier((p5, p4, p6, acc))
    s5 = send(p5, None, C)
    s4 = send(p4, None, C)
    (grads,) = call(
        functools.partial(last_kernel, width),
        [((wide + 8, embed), F32)],
        [flags, scal, w_m, w_o, z_m, zf, r, acc, stats, zo_a, zo_b, zo_c, mine, p1, p7, p6, s5, p5, s4, p4],
        [
            ((2, *wide_sq), BF16), ((2 * rows, wide), BF16), ((2 * rows, wide), BF16), (two, BF16), (two, F32),
            ((rows, 128), F32), ((4, *two), BF16), (two, F32), (stat, F32), (wide_sq, F32),
        ],
        14,
        20 * unit,
    )

    half = wide // 8
    g = [grads[k * half:(k + 1) * half] for k in range(8)]
    got = both(jnp.concatenate([g[2], g[3], g[6], g[7], grads[8 * half:]], axis=0), C)
    own_y, own_n, x_y, x_n = (a + got[k * half:(k + 1) * half] for k, a in enumerate((g[0], g[1], g[4], g[5])))
    tail = grads[8 * half:, 0] + got[4 * half:, 0]
    power = jnp.floor(14.0 - jnp.log2(tail[0] + 1e-30))
    scalars = tail[1:4] * (1.0 / 64)
    came = [decode(both(encode(v, power, scalars), flip)) for v, flip in ((x_y, X), (own_n, Y), (x_n, X | Y))]
    total = (own_y + came[0][0]) + (came[1][0] + came[2][0])
    scalars = (scalars + came[0][2]) + (came[1][2] + came[2][2])
    power = jnp.minimum(jnp.minimum(power, came[0][1]), jnp.minimum(came[1][1], came[2][1])) - 2
    flip = ZH
    while flip < n:
        message = encode(total, power, scalars)
        mine_v, mine_p, mine_s = decode(message)
        other_v, other_p, other_s = decode(both(message, flip))
        total, power, scalars = mine_v + other_v, jnp.minimum(mine_p, other_p) - 1, mine_s + other_s
        flip *= 2
    message = encode(total, power, scalars)
    here = [decode(message), decode(both(message, Y))]
    there = [decode(both(message, ZL)), decode(both(message, ZL | Y))]

    def order(v):
        return jnp.concatenate([jnp.where(y == 0, v[0][0], v[1][0]), jnp.where(y == 0, v[1][0], v[0][0])], axis=0)

    sums = jnp.where(images, here[0][2], there[0][2]) * (64.0 / (rows * n))
    here, there = order(here), order(there)
    return (sums[0], sums[2], sums[1], jnp.where(images, here, there), jnp.where(images, there, here))


def solution(mesh):
    return jax.shard_map(
        functools.partial(per_device, mesh.shape["batch"]),
        mesh=mesh,
        in_specs=(
            P(AXES, None),
            P(AXES, None),
            P("mp", None),
            P("mp", None),
            P(),
            P(),
        ),
        out_specs=(P(), P(), P(), P("mp", None), P("mp", None)),
        check_vma=False,
    )
```

```python
import functools

import jax
import jax.numpy as jnp
from jax import lax
from jax.experimental import pallas as pl
from jax.experimental.pallas import tpu as pltpu
from jax.sharding import PartitionSpec as P

AXES = ("batch", "mp")
LOG2E = 1.4426950408889634
STEP = 256
F32 = jnp.float32
F16 = jnp.float16
BF16 = jnp.bfloat16
C, X, Y, ZL, ZH = 1, 2, 4, 8, 16
ANY = pl.BlockSpec(memory_space=pl.ANY)
SMEM = pl.BlockSpec(memory_space=pltpu.SMEM)
VMEM = pl.BlockSpec(memory_space=pltpu.VMEM)


def is_home(i):
    b, m = divmod(i, 4)
    return m & 1 == b >> 2 & 1


def pairs(n, home, away):
    flips = [home if is_home(i) else away for i in range(n)]
    return [(i, i ^ f) for i, f in enumerate(flips) if f is not None]


def normalize(u):
    r = lax.rsqrt(jnp.sum(u * u, axis=1, keepdims=True) + 1e-06)
    return u * r, r


def project(feat, w):
    return normalize(jnp.dot(feat, w, preferred_element_type=F32))


def fold(v):
    return jnp.sum(v.reshape(v.shape[0] // 8, 8, v.shape[1]), axis=0)


def fetch(flags, pair, dst, sem):
    if not isinstance(pair, tuple):
        copy = pltpu.make_async_copy(pair, dst, sem)
        copy.start()
        return copy
    first, second = (pltpu.make_async_copy(p, dst, sem) for p in pair)

    @pl.when(flags[0] == 1)
    def _():
        first.start()

    @pl.when(flags[0] != 1)
    def _():
        second.start()

    return first


def pair_terms(scal, z_m, lo, hi, zo, acc, stats):
    a = scal[0] * LOG2E
    b = scal[1] * LOG2E

    def sims(i):
        return lax.dot_general(z_m[i:i + STEP, :], zo, (((1,), (1,)), ((), ())), preferred_element_type=F32)

    s = sims(lo)
    for i in range(lo, hi, STEP):
        ahead = sims(i + STEP) if i + STEP < hi else None
        t = jnp.exp2(s * a + b)
        d = 1.0 + t
        sig = t * pltpu.reciprocal(d, approx=False)
        q = STEP // 4
        d4 = (d[:q] * d[q:2 * q]) * (d[2 * q:3 * q] * d[3 * q:])
        stats[0] += fold(jnp.log(d4))
        stats[1] += fold(sig)
        stats[2] += fold(sig * s)
        acc[i:i + STEP, :] += jnp.dot(sig.astype(BF16), zo, preferred_element_type=F32)
        s = ahead


def first_kernel(flags, scal, w0, w1, w2, w3, m_h, m_a, o0_h, o0_a, o1_h, o1_a,
                 w_m, w_o, z_m, zf, r_out, acc, z_o, stats, w_in, f_in, sems):
    rows = f_in.shape[0] // 3
    part = w0.shape[0] // 2
    m = flags[1]
    copies = [fetch(flags, w, w_in.at[j], sems.at[j]) for j, w in enumerate((w0, w1, w2, w3))]
    copies += [
        fetch(flags, p, f_in.at[pl.ds(k * rows, rows), :], sems.at[4 + k])
        for k, p in enumerate(((m_h, m_a), (o0_h, o0_a), (o1_h, o1_a)))
    ]
    acc[...] = jnp.zeros_like(acc)
    stats[...] = jnp.zeros_like(stats)
    for j in range(4):
        copies[j].wait()
        at = pl.multiple_of((m ^ j) * part, part)
        w_m[pl.ds(at, part), :] = w_in[j, :part, :]
        w_o[pl.ds(at, part), :] = w_in[j, part:, :]
    copies[4].wait()
    zf_m, r = project(f_in[:rows, :], w_m[...])
    zf[...] = zf_m
    r_out[...] = jnp.broadcast_to(r, r_out.shape)
    z_m[...] = zf_m.astype(BF16)
    for k in range(2):
        copies[5 + k].wait()
        z_o[k * rows:(k + 1) * rows, :] = project(f_in[(k + 1) * rows:(k + 2) * rows, :], w_o[...])[0].astype(BF16)
    pair_terms(scal, z_m, 0, rows, z_o[...], acc, stats)


def next_kernel(flags, scal, w_o, z_m, acc_in, stats_in, o0_h, o0_a, o1_h, o1_a, acc, z_o, stats, w_in, f_in, z_in, sems):
    rows = z_in.shape[0]
    copies = [fetch(flags, w_o, w_in, sems.at[0])]
    copies += [
        fetch(flags, p, f_in.at[pl.ds(k * rows, rows), :], sems.at[1 + k])
        for k, p in enumerate(((o0_h, o0_a), (o1_h, o1_a)))
    ]
    copies += [
        fetch(flags, z_m, z_in, sems.at[3]),
        fetch(flags, acc_in, acc, sems.at[4]),
        fetch(flags, stats_in, stats, sems.at[5]),
    ]
    copies[0].wait()
    for k in range(2):
        copies[1 + k].wait()
        z_o[k * rows:(k + 1) * rows, :] = project(f_in[k * rows:(k + 1) * rows, :], w_in[...])[0].astype(BF16)
    for k in range(3, 6):
        copies[k].wait()
    pair_terms(scal, z_in, 0, rows, z_o[...], acc, stats)


def last_kernel(width, flags, scal, w_m, w_o, z_m, zf_m, r_m, acc_in, stats_in, zo_a, zo_b, zo_c, m0_h, m0_a, m1_h, m1_a,
                o0_h, o0_a, o1_h, o1_a, g_send, g_0, g_1, g_2, g_3, tail, w_in, feat, f_in, z, zf, r, z_o, acc, stats, grad, sems):
    rows = zf_m.shape[0]
    home, m, y = flags[0], flags[1], flags[2]
    scale, bias = scal[0], scal[1]

    def span(k):
        return pl.ds(k * rows, rows)

    def get(k, src, dst):
        return fetch(flags, src, dst, sems.at[k])

    c_wm = get(0, w_m, w_in.at[0])
    c_m1 = get(1, (m1_h, m1_a), feat.at[span(1), :])
    c_zo = [get(2 + k, v, z_o.at[k]) for k, v in enumerate((zo_a, zo_b, zo_c))]
    c_wo = get(5, w_o, w_in.at[1])
    c_o = [get(6 + k, p, f_in.at[span(k), :]) for k, p in enumerate(((o0_h, o0_a), (o1_h, o1_a)))]
    c_st = get(8, stats_in, stats)
    c_z = get(9, z_m, z.at[span(0), :])
    c_acc = get(10, acc_in, acc.at[span(0), :])
    c_zf = get(11, zf_m, zf.at[span(0), :])
    c_r = get(12, r_m, r)
    c_m0 = get(13, (m0_h, m0_a), feat.at[span(0), :])
    acc[rows:, :] = jnp.zeros_like(acc[rows:, :])
    c_wm.wait()
    c_m1.wait()
    zf_1, r_1 = project(feat[rows:, :], w_in[0])
    zf[rows:, :] = zf_1
    z[rows:, :] = zf_1.astype(BF16)
    c_st.wait()
    for k in range(3):
        c_zo[k].wait()
        pair_terms(scal, z, rows, 2 * rows, z_o[k], acc, stats)
    c_wo.wait()
    for k in range(2):
        c_o[k].wait()
        z_o[3, k * rows:(k + 1) * rows, :] = project(f_in[k * rows:(k + 1) * rows, :], w_in[1])[0].astype(BF16)
    c_z.wait()
    c_acc.wait()
    pair_terms(scal, z, 0, 2 * rows, z_o[3], acc, stats)
    c_zf.wait()
    c_r.wait()
    c_m0.wait()

    def finish(k, r_k, z_own):
        at = slice(k * rows, (k + 1) * rows)
        z_own = z_own.astype(F32)
        s = jnp.sum(z[at, :].astype(F32) * z_own, axis=1, keepdims=True)
        l = scale * s + bias
        t = jnp.exp2(s * (scale * LOG2E) + bias * LOG2E)
        rest = pltpu.reciprocal(1.0 + t, approx=False)
        change = (-rest).astype(BF16).astype(F32) - (t * rest).astype(BF16).astype(F32)
        dz = (scale / width) * (acc[at, :] + change * z_own)
        zf_k = zf[at, :]
        du = (r_k * (dz - zf_k * jnp.sum(zf_k * dz, axis=1, keepdims=True))).astype(BF16)
        return du, jnp.sum(s), jnp.sum(l)

    own_0 = jnp.where(home == 1, z_o[0, :rows, :], z_o[2, :rows, :])
    own_1 = jnp.where(home == 1, z_o[0, rows:, :], z_o[1, :rows, :])
    du_0, s_0, l_0 = finish(0, r[:, :1], own_0)
    du_1, s_1, l_1 = finish(1, r_1, own_1)
    grad[...] = lax.dot_general(
        feat[...], jnp.concatenate([du_0, du_1], axis=0), (((0,), (0,)), ((), ())), preferred_element_type=F32
    )
    half = grad.shape[0] // 8

    def piece(j, h):
        return grad[pl.ds(pl.multiple_of((m ^ j) * 2 * half + (y ^ h) * half, half), half), :]

    for k, (j, h) in enumerate(((0, 0), (0, 1), (2, 0), (2, 1))):
        g_send[k * half:(k + 1) * half, :] = piece(j ^ 1, h)
        (g_0, g_1, g_2, g_3)[k][...] = piece(j, h)
    most = jnp.max(jnp.abs(grad[...]))
    loss = (jnp.sum(stats[0]) - (l_0 + l_1)) / width
    gsum = (jnp.sum(stats[1]) - 2 * rows) / width
    gscale = scale * (jnp.sum(stats[2]) - (s_0 + s_1)) / width
    row = lax.broadcasted_iota(jnp.int32, tail.shape, 0)
    values = jnp.zeros(tail.shape, F32)
    for k, v in enumerate((most, loss, gsum, gscale)):
        values = jnp.where(row == k, v, values)
    tail[...] = values


def call(kernel, outs, inputs, scratch, sems, flops):
    def spec(v):
        return SMEM if v.ndim == 1 else ANY

    return pl.pallas_call(
        kernel,
        out_shape=[jax.ShapeDtypeStruct(*o) for o in outs],
        in_specs=[spec(v) for v in inputs],
        out_specs=[VMEM] * len(outs),
        scratch_shapes=[pltpu.VMEM(*s) for s in scratch] + [pltpu.SemaphoreType.DMA((sems,))],
        compiler_params=pltpu.CompilerParams(vmem_limit_bytes=48 * 2**20),
        cost_estimate=pl.CostEstimate(flops=flops, bytes_accessed=1, transcendentals=0),
    )(*inputs)


def encode(values, tail):
    return (values * (16384.0 / (tail[:1] + 1e-30))).astype(F16)


def decode(message, tail):
    return message.astype(F32) * ((tail[:1] + 1e-30) * (1.0 / 16384.0))


def per_device(n_batch, img_feat, txt_feat, img_proj, txt_proj, logit_scale, bias):
    rows, wide = img_feat.shape
    embed = img_proj.shape[1]
    n = n_batch * 4
    width = 8 * rows
    b = lax.axis_index("batch")
    m = lax.axis_index("mp")
    y, zl, zh, c = b & 1, b >> 1 & 1, b >> 2 & 1, m & 1
    home = (c == zh).astype(jnp.int32)
    images = zl == 0
    flags = jnp.stack([home, m, y])
    scal = jnp.stack([jnp.exp(logit_scale), bias])

    def send(v, home, away, name):
        with jax.named_scope(name):
            return lax.ppermute(v, AXES, pairs(n, home, away))

    def both(v, flip, name):
        return send(v, flip, flip, name)

    swap = ZH | C
    mine = jnp.where(images, img_feat, txt_feat)
    opp = jnp.where(images, txt_feat, img_feat)
    w0 = jnp.concatenate([jnp.where(images, img_proj, txt_proj), jnp.where(images, txt_proj, img_proj)], axis=0)
    p1 = send(mine, ZL, swap, "mine_swap")
    w2 = both(w0, X, "proj_x")
    w1 = both(w0, C, "proj_core")
    s0 = send(opp, C, None, "sib0")
    p1, w2, opp_late = lax.optimization_barrier((p1, w2, opp))
    p2 = send(opp_late, Y, swap, "opp_swap")
    p3 = send(p1, Y, ZL, "mine_square")
    w3 = both(w2, C, "proj_xcore")
    s1 = send(p1, C, None, "sib1")
    p7 = send(opp, ZL, None, "opp_home_z")

    wide_sq = (wide, embed)
    two = (2 * rows, embed)
    one = (rows, embed)
    stat = (3, 8, 2 * rows)
    unit = 2 * rows * rows * embed
    w_m, w_o, z_m, zf, r, acc, zo_a, stats = call(
        first_kernel,
        [(wide_sq, BF16), (wide_sq, BF16), (one, BF16), (one, F32), ((rows, 128), F32), (one, F32), (two, BF16), (stat, F32)],
        [flags, scal, w0, w1, w2, w3, mine, p1, opp, s0, p1, s1],
        [((4, *w0.shape), BF16), ((3 * rows, wide), BF16)],
        7,
        1,
    )

    def middle(z_m, acc, stats, o0_h, o0_a, o1_h, o1_a):
        return call(
            next_kernel,
            [(one, F32), (two, BF16), (stat, F32)],
            [flags, scal, w_o, z_m, acc, stats, o0_h, o0_a, o1_h, o1_a],
            [(wide_sq, BF16), ((2 * rows, wide), BF16), (one, BF16)],
            6,
            1,
        )

    p2, p3, acc = lax.optimization_barrier((p2, p3, acc))
    s3 = both(p3, C, "sib3")
    p5 = send(p3, None, Y, "mine_square_y")
    acc, zo_b, stats = middle(z_m, acc, stats, p3, p3, s3, s3)
    p4 = send(p2, None, Y, "opp_square_y")
    p6 = send(p2, None, ZL, "opp_square_z")
    s2 = both(p2, C, "sib2")
    acc, zo_c, stats = middle(z_m, acc, stats, p2, p2, s2, s2)
    p5, p4, p6, acc = lax.optimization_barrier((p5, p4, p6, acc))
    s5 = send(p5, None, C, "sib5")
    s4 = send(p4, None, C, "sib4")
    half = wide // 8
    pieces, *kept, tail = call(
        functools.partial(last_kernel, width),
        [((4 * half, embed), F32)] + [((half, embed), F32)] * 4 + [((8, embed), F32)],
        [flags, scal, w_m, w_o, z_m, zf, r, acc, stats, zo_a, zo_b, zo_c, mine, p1, p7, p6, s5, p5, s4, p4],
        [
            ((2, *wide_sq), BF16), ((2 * rows, wide), BF16), ((2 * rows, wide), BF16), (two, BF16), (two, F32),
            ((rows, 128), F32), ((4, *two), BF16), (two, F32), (stat, F32), (wide_sq, F32),
        ],
        14,
        1,
    )

    got, more = lax.optimization_barrier((both(pieces, C, "core_sum"), both(tail, C, "core_sum")))
    tail = tail + more
    kept = [v + got[k * half:(k + 1) * half] for k, v in enumerate(kept)]
    messages = lax.optimization_barrier(tuple(encode(v, tail) for v in kept[1:]) + (tail,))
    tail = messages[3]
    ways = (Y, X, X | Y)
    came = tuple(both(v, flip, "square_sum") for v, flip in zip(messages, ways))
    came = came + tuple(both(tail, flip, "square_sum") for flip in ways)
    came = lax.optimization_barrier(came)
    parts = [decode(v, t) for v, t in zip(came[:3], came[3:])]
    total = (kept[0] + parts[0]) + (parts[1] + parts[2])
    tail = (tail + came[3]) + (came[4] + came[5])
    flip = ZH
    while flip < n:
        message, tail = lax.optimization_barrier((encode(total, tail), tail))
        other, more = lax.optimization_barrier((both(message, flip, "half_sum"), both(tail, flip, "half_sum")))
        total = decode(message, tail) + decode(other, more)
        tail = tail + more
        flip *= 2
    message, tail = lax.optimization_barrier((encode(total, tail), tail))
    by_y, by_z, by_yz, more = lax.optimization_barrier((
        both(message, Y, "hand_out"),
        both(message, ZL, "hand_out"),
        both(message, ZL | Y, "hand_out"),
        both(tail, ZL, "hand_out"),
    ))

    def order(first, second, t):
        first, second = decode(first, t), decode(second, t)
        return jnp.concatenate([jnp.where(y == 0, first, second), jnp.where(y == 0, second, first)], axis=0)

    here, there = order(message, by_y, tail), order(by_z, by_yz, more)
    sums = jnp.where(images, tail, more)[:, 0] / (rows * n)
    return (sums[1], sums[3], sums[2], jnp.where(images, here, there), jnp.where(images, there, here))


def solution(mesh):
    return jax.shard_map(
        functools.partial(per_device, mesh.shape["batch"]),
        mesh=mesh,
        in_specs=(
            P(AXES, None),
            P(AXES, None),
            P("mp", None),
            P("mp", None),
            P(),
            P(),
        ),
        out_specs=(P(), P(), P(), P("mp", None), P("mp", None)),
        check_vma=False,
    )
```

```python
import functools

import jax
import jax.numpy as jnp
from jax import lax
from jax.experimental import pallas as pl
from jax.experimental.pallas import tpu as pltpu
from jax.sharding import PartitionSpec as P

AXES = ("batch", "mp")
LOG2E = 1.4426950408889634
STEP = 256
LANES = 512
F32 = jnp.float32
F16 = jnp.float16
BF16 = jnp.bfloat16
C, X, ROLE, SIDE, ZH = 1, 2, 4, 8, 16
ANY = pl.BlockSpec(memory_space=pl.ANY)
SMEM = pl.BlockSpec(memory_space=pltpu.SMEM)
VMEM = pl.BlockSpec(memory_space=pltpu.VMEM)


def is_home(i):
    b, m = divmod(i, 4)
    return m & 1 == b >> 2 & 1


def pairs(n, home, away):
    flips = [home if is_home(i) else away for i in range(n)]
    return [(i, i ^ f) for i, f in enumerate(flips) if f is not None]


def normalize(u):
    r = lax.rsqrt(jnp.sum(u * u, axis=1, keepdims=True) + 1e-06)
    return u * r, r


def project(feat, w):
    return normalize(jnp.dot(feat, w, preferred_element_type=F32))


def fold(v):
    v = jnp.sum(v.reshape(v.shape[0] // 8, 8, v.shape[1]), axis=0)
    return sum(v[:, k:k + LANES] for k in range(0, v.shape[1], LANES))


def fetch(flags, pair, dst, sem):
    if not isinstance(pair, tuple):
        copy = pltpu.make_async_copy(pair, dst, sem)
        copy.start()
        return copy
    first, second = (pltpu.make_async_copy(p, dst, sem) for p in pair)

    @pl.when(flags[0] == 1)
    def _():
        first.start()

    @pl.when(flags[0] != 1)
    def _():
        second.start()

    return first


def pair_terms(scal, z_m, lo, hi, zo, acc, stats):
    a = scal[0] * LOG2E
    b = scal[1] * LOG2E

    def sims(i):
        return lax.dot_general(z_m[i:i + STEP, :], zo, (((1,), (1,)), ((), ())), preferred_element_type=F32)

    s = sims(lo)
    for i in range(lo, hi, STEP):
        ahead = sims(i + STEP) if i + STEP < hi else None
        t = jnp.exp2(s * a + b)
        d = 1.0 + t
        sig = t * pltpu.reciprocal(d, approx=False)
        q = STEP // 4
        d4 = (d[:q] * d[q:2 * q]) * (d[2 * q:3 * q] * d[3 * q:])
        stats[0] += fold(jnp.log(d4))
        stats[1] += fold(sig)
        stats[2] += fold(sig * s)
        acc[i:i + STEP, :] += jnp.dot(sig.astype(BF16), zo, preferred_element_type=F32)
        s = ahead


def first_kernel(flags, scal, w0, w1, w2, w3, m_h, m_a, o0_h, o0_a, o1_h, o1_a,
                 w_m, w_o, z_m, zf, r_out, acc, z_o, stats, w_in, f_in, sems):
    rows = f_in.shape[0] // 3
    part = w0.shape[0] // 2
    m = flags[1]
    copies = [fetch(flags, w, w_in.at[j], sems.at[j]) for j, w in enumerate((w0, w1, w2, w3))]
    copies += [
        fetch(flags, p, f_in.at[pl.ds(k * rows, rows), :], sems.at[4 + k])
        for k, p in enumerate(((m_h, m_a), (o0_h, o0_a), (o1_h, o1_a)))
    ]
    acc[...] = jnp.zeros_like(acc)
    stats[...] = jnp.zeros_like(stats)
    for j in range(4):
        copies[j].wait()
        at = pl.multiple_of((m ^ j) * part, part)
        w_m[pl.ds(at, part), :] = w_in[j, :part, :]
        w_o[pl.ds(at, part), :] = w_in[j, part:, :]
    copies[4].wait()
    zf_m, r = project(f_in[:rows, :], w_m[...])
    zf[...] = zf_m
    r_out[...] = jnp.broadcast_to(r, r_out.shape)
    z_m[...] = zf_m.astype(BF16)
    for k in range(2):
        copies[5 + k].wait()
        z_o[k * rows:(k + 1) * rows, :] = project(f_in[(k + 1) * rows:(k + 2) * rows, :], w_o[...])[0].astype(BF16)
    pair_terms(scal, z_m, 0, rows, z_o[...], acc, stats)


def embed_kernel(flags, w_o, o0, o1_h, o1_a, z_o, w_in, f_in, sems):
    rows = f_in.shape[0] // 2
    copies = [fetch(flags, w_o, w_in, sems.at[0])]
    copies += [fetch(flags, p, f_in.at[pl.ds(k * rows, rows), :], sems.at[1 + k]) for k, p in enumerate((o0, (o1_h, o1_a)))]
    copies[0].wait()
    for k in range(2):
        copies[1 + k].wait()
        z_o[k * rows:(k + 1) * rows, :] = project(f_in[k * rows:(k + 1) * rows, :], w_in[...])[0].astype(BF16)


def next_kernel(flags, scal, z_m, acc_in, stats_in, own, sibling, acc, stats, z_in, z_o, sems):
    rows = z_in.shape[0]
    copies = [
        fetch(flags, z_m, z_in, sems.at[0]),
        fetch(flags, own, z_o.at[pl.ds(0, 2 * rows), :], sems.at[1]),
        fetch(flags, sibling, z_o.at[pl.ds(2 * rows, 2 * rows), :], sems.at[2]),
        fetch(flags, acc_in, acc, sems.at[3]),
        fetch(flags, stats_in, stats, sems.at[4]),
    ]
    for c in copies:
        c.wait()
    pair_terms(scal, z_in, 0, rows, z_o[...], acc, stats)


def late_kernel(flags, scal, w_m, stats_in, zo_a, zo_b, zo_c, m1_h, m1_a, z_m, zf, r_out, acc, stats, w_in, f_in, z_o, sems):
    rows = f_in.shape[0]
    copies = [
        fetch(flags, w_m, w_in, sems.at[0]),
        fetch(flags, (m1_h, m1_a), f_in, sems.at[1]),
        fetch(flags, stats_in, stats, sems.at[2]),
    ]
    copies += [fetch(flags, v, z_o.at[pl.ds(2 * k * rows, 2 * rows), :], sems.at[3 + k]) for k, v in enumerate((zo_a, zo_b, zo_c))]
    acc[...] = jnp.zeros_like(acc)
    copies[0].wait()
    copies[1].wait()
    zf_m, r = project(f_in[...], w_in[...])
    zf[...] = zf_m
    r_out[...] = jnp.broadcast_to(r, r_out.shape)
    z_m[...] = zf_m.astype(BF16)
    for c in copies[2:]:
        c.wait()
    pair_terms(scal, z_m, 0, rows, z_o[:3 * rows, :], acc, stats)
    pair_terms(scal, z_m, 0, rows, z_o[3 * rows:, :], acc, stats)


def last_kernel(width, flags, scal, z_0, z_1, zf_0, zf_1, r_0, r_1, acc_0, acc_1, stats_in, zo_a, zo_b,
                m0_h, m0_a, m1_h, m1_a, o_h, o_a,
                g_send, g_0, g_1, g_2, g_3, tail, feat, z, zf, r, z_o, z_own, acc, stats, grad, sems):
    rows = r.shape[0] // 2
    home, m, side = flags[0], flags[1], flags[2]
    scale, bias = scal[0], scal[1]

    def span(k):
        return pl.ds(k * rows, rows)

    def get(k, src, dst):
        return fetch(flags, src, dst, sems.at[k])

    now = [get(k, v, z.at[span(k), :]) for k, v in enumerate((z_0, z_1))]
    now += [get(2, (o_h, o_a), z_o), get(3, stats_in, stats)]
    now += [get(4 + k, v, acc.at[span(k), :]) for k, v in enumerate((acc_0, acc_1))]
    rest = [get(6 + k, v, zf.at[span(k), :]) for k, v in enumerate((zf_0, zf_1))]
    rest += [get(8 + k, v, r.at[span(k), :]) for k, v in enumerate((r_0, r_1))]
    rest += [get(10 + k, v, feat.at[span(k), :]) for k, v in enumerate(((m0_h, m0_a), (m1_h, m1_a)))]
    first = (zo_a.at[span(0), :], zo_b.at[span(1), :])
    second = (zo_a.at[span(1), :], zo_b.at[span(0), :])
    rest += [get(12 + k, v, z_own.at[span(k), :]) for k, v in enumerate((first, second))]
    for c in now:
        c.wait()
    pair_terms(scal, z, 0, 2 * rows, z_o[...], acc, stats)
    for c in rest:
        c.wait()

    def finish(k):
        at = slice(k * rows, (k + 1) * rows)
        pair = z_own[at, :].astype(F32)
        s = jnp.sum(z[at, :].astype(F32) * pair, axis=1, keepdims=True)
        l = scale * s + bias
        t = jnp.exp2(s * (scale * LOG2E) + bias * LOG2E)
        rest = pltpu.reciprocal(1.0 + t, approx=False)
        change = (-rest).astype(BF16).astype(F32) - (t * rest).astype(BF16).astype(F32)
        dz = (scale / width) * (acc[at, :] + change * pair)
        zf_k = zf[at, :]
        du = (r[at, :1] * (dz - zf_k * jnp.sum(zf_k * dz, axis=1, keepdims=True))).astype(BF16)
        return du, jnp.sum(s), jnp.sum(l)

    du_0, s_0, l_0 = finish(0)
    du_1, s_1, l_1 = finish(1)
    grad[...] = lax.dot_general(
        feat[...], jnp.concatenate([du_0, du_1], axis=0), (((0,), (0,)), ((), ())), preferred_element_type=F32
    )
    half = grad.shape[0] // 8

    def piece(j, h):
        return grad[pl.ds(pl.multiple_of((m ^ j) * 2 * half + (side ^ h) * half, half), half), :]

    for k, (j, h) in enumerate(((0, 0), (0, 1), (2, 0), (2, 1))):
        g_send[k * half:(k + 1) * half, :] = piece(j ^ 1, h)
        (g_0, g_1, g_2, g_3)[k][...] = piece(j, h)
    most = jnp.max(jnp.abs(grad[...]))
    loss = (jnp.sum(stats[0]) - (l_0 + l_1)) / width
    gsum = (jnp.sum(stats[1]) - 2 * rows) / width
    gscale = scale * (jnp.sum(stats[2]) - (s_0 + s_1)) / width
    row = lax.broadcasted_iota(jnp.int32, tail.shape, 0)
    values = jnp.zeros(tail.shape, F32)
    for k, v in enumerate((most, loss, gsum, gscale)):
        values = jnp.where(row == k, v, values)
    tail[...] = values


def call(kernel, outs, inputs, scratch, sems, limit=32):
    def spec(v):
        return SMEM if v.ndim == 1 else ANY

    return pl.pallas_call(
        kernel,
        out_shape=[jax.ShapeDtypeStruct(*o) for o in outs],
        in_specs=[spec(v) for v in inputs],
        out_specs=[VMEM] * len(outs),
        scratch_shapes=[pltpu.VMEM(*s) for s in scratch] + [pltpu.SemaphoreType.DMA((sems,))],
        compiler_params=pltpu.CompilerParams(vmem_limit_bytes=limit * 2**20),
        cost_estimate=pl.CostEstimate(flops=1, bytes_accessed=1, transcendentals=0),
    )(*inputs)


def encode(values, tail):
    return (values * (16384.0 / (tail[:1] + 1e-30))).astype(F16)


def decode(message, tail):
    return message.astype(F32) * ((tail[:1] + 1e-30) * (1.0 / 16384.0))


def per_device(n_batch, img_feat, txt_feat, img_proj, txt_proj, logit_scale, bias):
    rows, wide = img_feat.shape
    embed = img_proj.shape[1]
    n = n_batch * 4
    width = 8 * rows
    b = lax.axis_index("batch")
    m = lax.axis_index("mp")
    role, side, zh, c = b & 1, b >> 1 & 1, b >> 2 & 1, m & 1
    home = (c == zh).astype(jnp.int32)
    images = role == 0
    flags = jnp.stack([home, m, side])
    scal = jnp.stack([jnp.exp(logit_scale), bias])

    def send(v, home, away, name):
        with jax.named_scope(name):
            return lax.ppermute(v, AXES, pairs(n, home, away))

    def both(v, flip, name):
        return send(v, flip, flip, name)

    swap = ZH | C
    mine = jnp.where(images, img_feat, txt_feat)
    opp = jnp.where(images, txt_feat, img_feat)
    w0 = jnp.concatenate([jnp.where(images, img_proj, txt_proj), jnp.where(images, txt_proj, img_proj)], axis=0)
    p1 = send(mine, ROLE, swap, "mine_swap")
    w2 = both(w0, X, "proj_x")
    w1 = both(w0, C, "proj_core")
    s0 = send(opp, C, None, "sib_opp")
    p0 = send(opp, SIDE, None, "opp_home_side")
    w3 = both(w2, C, "proj_xcore")
    p1, w2, opp_late, p0 = lax.optimization_barrier((p1, w2, opp, p0))
    p2 = send(opp_late, ROLE, swap, "opp_swap")
    p3 = send(p1, SIDE, ROLE, "mine_square")
    s1 = send(p1, C, None, "sib_mine")

    square = (wide, embed)
    one, two = (rows, embed), (2 * rows, embed)
    norm = (rows, 128)
    stat = (3, 8, LANES)
    w_m, w_o, z_0, zf_0, r_0, acc_0, zo_a, stats = call(
        first_kernel,
        [(square, BF16), (square, BF16), (one, BF16), (one, F32), (norm, F32), (one, F32), (two, BF16), (stat, F32)],
        [flags, scal, w0, w1, w2, w3, mine, p1, opp, s0, p1, s1],
        [((4, *w0.shape), BF16), ((3 * rows, wide), BF16)],
        7,
    )
    p2, p3, w_o = lax.optimization_barrier((p2, p3, w_o))
    p6 = send(p2, None, ROLE, "opp_square_role")
    (zo_b,) = call(embed_kernel, [(two, BF16)], [flags, w_o, p3, p0, p2], [(square, BF16), (two, BF16)], 3)
    zo_c = both(zo_b, C, "sib_square")
    p4 = send(zo_b, None, SIDE, "square_side")
    acc_0, stats = call(
        next_kernel,
        [(one, F32), (stat, F32)],
        [flags, scal, z_0, acc_0, stats, zo_b, zo_c],
        [(one, BF16), ((4 * rows, embed), BF16)],
        5,
    )
    p6, acc_0, stats = lax.optimization_barrier((p6, acc_0, stats))
    z_1, zf_1, r_1, acc_1, stats = call(
        late_kernel,
        [(one, BF16), (one, F32), (norm, F32), (one, F32), (stat, F32)],
        [flags, scal, w_m, stats, zo_a, zo_b, zo_c, p2, p6],
        [(square, BF16), (one, BF16), ((6 * rows, embed), BF16)],
        6,
    )
    p4, acc_1 = lax.optimization_barrier((p4, acc_1))
    s4 = send(p4, None, C, "sib_side")
    half = wide // 8
    pieces, *kept, tail = call(
        functools.partial(last_kernel, width),
        [((4 * half, embed), F32)] + [((half, embed), F32)] * 4 + [((8, embed), F32)],
        [flags, scal, z_0, z_1, zf_0, zf_1, r_0, r_1, acc_0, acc_1, stats, zo_a, zo_b, mine, p1, p2, p6, s4, p4],
        [
            (two, BF16), (two, BF16), (two, F32), ((2 * rows, 128), F32), (two, BF16), (two, BF16), (two, F32),
            (stat, F32), (square, F32),
        ],
        14,
    )

    got, more = lax.optimization_barrier((both(pieces, C, "core_sum"), both(tail, C, "core_sum")))
    tail = tail + more
    kept = [v + got[k * half:(k + 1) * half] for k, v in enumerate(kept)]
    messages = lax.optimization_barrier(tuple(encode(v, tail) for v in kept[1:]) + (tail,))
    tail = messages[3]
    ways = (SIDE, X, X | SIDE)
    came = tuple(both(v, flip, "square_sum") for v, flip in zip(messages, ways))
    came = came + tuple(both(tail, flip, "square_sum") for flip in ways)
    came = lax.optimization_barrier(came)
    parts = [decode(v, t) for v, t in zip(came[:3], came[3:])]
    total = (kept[0] + parts[0]) + (parts[1] + parts[2])
    tail = (tail + came[3]) + (came[4] + came[5])
    flip = ZH
    while flip < n:
        message, tail = lax.optimization_barrier((encode(total, tail), tail))
        other, more = lax.optimization_barrier((both(message, flip, "half_sum"), both(tail, flip, "half_sum")))
        total = decode(message, tail) + decode(other, more)
        tail = tail + more
        flip *= 2
    message, tail = lax.optimization_barrier((encode(total, tail), tail))
    by_s, by_r, by_rs, more = lax.optimization_barrier((
        both(message, SIDE, "hand_out"),
        both(message, ROLE, "hand_out"),
        both(message, ROLE | SIDE, "hand_out"),
        both(tail, ROLE, "hand_out"),
    ))

    def order(first, second, t):
        first, second = decode(first, t), decode(second, t)
        return jnp.concatenate([jnp.where(side == 0, first, second), jnp.where(side == 0, second, first)], axis=0)

    here, there = order(message, by_s, tail), order(by_r, by_rs, more)
    sums = jnp.where(images, tail, more)[:, 0] / (rows * n)
    return (sums[1], sums[3], sums[2], jnp.where(images, here, there), jnp.where(images, there, here))


def solution(mesh):
    return jax.shard_map(
        functools.partial(per_device, mesh.shape["batch"]),
        mesh=mesh,
        in_specs=(
            P(AXES, None),
            P(AXES, None),
            P("mp", None),
            P("mp", None),
            P(),
            P(),
        ),
        out_specs=(P(), P(), P(), P("mp", None), P("mp", None)),
        check_vma=False,
    )
```

```python
import functools

import jax
import jax.numpy as jnp
from jax import lax
from jax.experimental import pallas as pl
from jax.experimental.pallas import tpu as pltpu
from jax.sharding import PartitionSpec as P

AXES = ("batch", "mp")
LOG2E = 1.4426950408889634
STEP = 256
LANES = 512
F32 = jnp.float32
F16 = jnp.float16
BF16 = jnp.bfloat16
C, X, ROLE, SIDE, ZH = 1, 2, 4, 8, 16
ANY = pl.BlockSpec(memory_space=pl.ANY)
SMEM = pl.BlockSpec(memory_space=pltpu.SMEM)
VMEM = pl.BlockSpec(memory_space=pltpu.VMEM)


def is_home(i):
    b, m = divmod(i, 4)
    return m & 1 == b >> 2 & 1


def pairs(n, home, away):
    flips = [home if is_home(i) else away for i in range(n)]
    return [(i, i ^ f) for i, f in enumerate(flips) if f is not None]


def normalize(u):
    r = lax.rsqrt(jnp.sum(u * u, axis=1, keepdims=True) + 1e-06)
    return u * r, r


def project(feat, w):
    return normalize(jnp.dot(feat, w, preferred_element_type=F32))


def fold(v):
    v = jnp.sum(v.reshape(v.shape[0] // 8, 8, v.shape[1]), axis=0)
    return sum(v[:, k:k + LANES] for k in range(0, v.shape[1], LANES))


def fetch(flags, pair, dst, sem):
    if not isinstance(pair, tuple):
        copy = pltpu.make_async_copy(pair, dst, sem)
        copy.start()
        return copy
    first, second = (pltpu.make_async_copy(p, dst, sem) for p in pair)

    @pl.when(flags[0] == 1)
    def _():
        first.start()

    @pl.when(flags[0] != 1)
    def _():
        second.start()

    return first


def pair_terms(scal, z_m, lo, hi, zo, acc, stats):
    a = scal[0] * LOG2E
    b = scal[1] * LOG2E

    def sims(i):
        return lax.dot_general(z_m[i:i + STEP, :], zo, (((1,), (1,)), ((), ())), preferred_element_type=F32)

    s = sims(lo)
    for i in range(lo, hi, STEP):
        ahead = sims(i + STEP) if i + STEP < hi else None
        t = jnp.exp2(s * a + b)
        d = 1.0 + t
        sig = t * pltpu.reciprocal(d, approx=False)
        q = STEP // 4
        d4 = (d[:q] * d[q:2 * q]) * (d[2 * q:3 * q] * d[3 * q:])
        stats[0] += fold(jnp.log(d4))
        stats[1] += fold(sig)
        stats[2] += fold(sig * s)
        acc[i:i + STEP, :] += jnp.dot(sig.astype(BF16), zo, preferred_element_type=F32)
        s = ahead


def first_kernel(flags, scal, w0, w1, w2, w3, m_h, m_a, o0_h, o0_a, o1_h, o1_a,
                 w_m, w_o, z_m, zf, r_out, acc, z_o, stats, w_in, f_in, sems):
    rows = f_in.shape[0] // 3
    part = w0.shape[0] // 2
    m = flags[1]
    copies = [fetch(flags, w, w_in.at[j], sems.at[j]) for j, w in enumerate((w0, w1, w2, w3))]
    copies += [
        fetch(flags, p, f_in.at[pl.ds(k * rows, rows), :], sems.at[4 + k])
        for k, p in enumerate(((m_h, m_a), (o0_h, o0_a), (o1_h, o1_a)))
    ]
    acc[...] = jnp.zeros_like(acc)
    stats[...] = jnp.zeros_like(stats)
    for j in range(4):
        copies[j].wait()
        at = pl.multiple_of((m ^ j) * part, part)
        w_m[pl.ds(at, part), :] = w_in[j, :part, :]
        w_o[pl.ds(at, part), :] = w_in[j, part:, :]
    copies[4].wait()
    zf_m, r = project(f_in[:rows, :], w_m[...])
    zf[...] = zf_m
    r_out[...] = jnp.broadcast_to(r, r_out.shape)
    z_m[...] = zf_m.astype(BF16)
    for k in range(2):
        copies[5 + k].wait()
        z_o[k * rows:(k + 1) * rows, :] = project(f_in[(k + 1) * rows:(k + 2) * rows, :], w_o[...])[0].astype(BF16)
    pair_terms(scal, z_m, 0, rows, z_o[...], acc, stats)


def embed_kernel(flags, w_o, o0, o1_h, o1_a, z_o, w_in, f_in, sems):
    rows = f_in.shape[0] // 2
    copies = [fetch(flags, w_o, w_in, sems.at[0])]
    copies += [fetch(flags, p, f_in.at[pl.ds(k * rows, rows), :], sems.at[1 + k]) for k, p in enumerate((o0, (o1_h, o1_a)))]
    copies[0].wait()
    for k in range(2):
        copies[1 + k].wait()
        z_o[k * rows:(k + 1) * rows, :] = project(f_in[k * rows:(k + 1) * rows, :], w_in[...])[0].astype(BF16)


def next_kernel(flags, scal, z_m, acc_in, stats_in, own, sibling, acc, stats, z_in, z_o, sems):
    rows = z_in.shape[0]
    copies = [
        fetch(flags, z_m, z_in, sems.at[0]),
        fetch(flags, own, z_o.at[pl.ds(0, 2 * rows), :], sems.at[1]),
        fetch(flags, sibling, z_o.at[pl.ds(2 * rows, 2 * rows), :], sems.at[2]),
        fetch(flags, acc_in, acc, sems.at[3]),
        fetch(flags, stats_in, stats, sems.at[4]),
    ]
    for c in copies:
        c.wait()
    pair_terms(scal, z_in, 0, rows, z_o[...], acc, stats)


def late_kernel(flags, scal, w_m, stats_in, zo_a, zo_b, zo_c, m1_h, m1_a, z_m, zf, r_out, acc, stats, w_in, f_in, z_o, sems):
    rows = f_in.shape[0]
    copies = [
        fetch(flags, w_m, w_in, sems.at[0]),
        fetch(flags, (m1_h, m1_a), f_in, sems.at[1]),
        fetch(flags, stats_in, stats, sems.at[2]),
    ]
    copies += [fetch(flags, v, z_o.at[pl.ds(2 * k * rows, 2 * rows), :], sems.at[3 + k]) for k, v in enumerate((zo_a, zo_b, zo_c))]
    acc[...] = jnp.zeros_like(acc)
    copies[0].wait()
    copies[1].wait()
    zf_m, r = project(f_in[...], w_in[...])
    zf[...] = zf_m
    r_out[...] = jnp.broadcast_to(r, r_out.shape)
    z_m[...] = zf_m.astype(BF16)
    for c in copies[2:]:
        c.wait()
    pair_terms(scal, z_m, 0, rows, z_o[:3 * rows, :], acc, stats)
    pair_terms(scal, z_m, 0, rows, z_o[3 * rows:, :], acc, stats)


def last_kernel(width, flags, scal, z_0, z_1, zf_0, zf_1, r_0, r_1, acc_0, acc_1, stats_in, zo_a, zo_b,
                m0_h, m0_a, m1_h, m1_a, o_h, o_a,
                g_send, g_0, g_1, g_2, g_3, tail, feat, z, zf, r, z_o, z_own, acc, stats, grad, sems):
    rows = r.shape[0] // 2
    home, m, side = flags[0], flags[1], flags[2]
    scale, bias = scal[0], scal[1]

    def span(k):
        return pl.ds(k * rows, rows)

    def get(k, src, dst):
        return fetch(flags, src, dst, sems.at[k])

    now = [get(k, v, z.at[span(k), :]) for k, v in enumerate((z_0, z_1))]
    now += [get(2, (o_h, o_a), z_o), get(3, stats_in, stats)]
    now += [get(4 + k, v, acc.at[span(k), :]) for k, v in enumerate((acc_0, acc_1))]
    rest = [get(6 + k, v, zf.at[span(k), :]) for k, v in enumerate((zf_0, zf_1))]
    rest += [get(8 + k, v, r.at[span(k), :]) for k, v in enumerate((r_0, r_1))]
    rest += [get(10 + k, v, feat.at[span(k), :]) for k, v in enumerate(((m0_h, m0_a), (m1_h, m1_a)))]
    first = (zo_a.at[span(0), :], zo_b.at[span(1), :])
    second = (zo_a.at[span(1), :], zo_b.at[span(0), :])
    rest += [get(12 + k, v, z_own.at[span(k), :]) for k, v in enumerate((first, second))]
    for c in now:
        c.wait()
    pair_terms(scal, z, 0, 2 * rows, z_o[...], acc, stats)
    for c in rest:
        c.wait()

    def finish(k):
        at = slice(k * rows, (k + 1) * rows)
        pair = z_own[at, :].astype(F32)
        s = jnp.sum(z[at, :].astype(F32) * pair, axis=1, keepdims=True)
        l = scale * s + bias
        t = jnp.exp2(s * (scale * LOG2E) + bias * LOG2E)
        rest = pltpu.reciprocal(1.0 + t, approx=False)
        change = (-rest).astype(BF16).astype(F32) - (t * rest).astype(BF16).astype(F32)
        dz = (scale / width) * (acc[at, :] + change * pair)
        zf_k = zf[at, :]
        du = (r[at, :1] * (dz - zf_k * jnp.sum(zf_k * dz, axis=1, keepdims=True))).astype(BF16)
        return du, jnp.sum(s), jnp.sum(l)

    def gradient(k, du):
        return lax.dot_general(feat[k * rows:(k + 1) * rows, :], du, (((0,), (0,)), ((), ())), preferred_element_type=F32)

    du_0, s_0, l_0 = finish(0)
    part_0 = gradient(0, du_0)
    du_1, s_1, l_1 = finish(1)
    grad[...] = part_0 + gradient(1, du_1)
    half = grad.shape[0] // 8

    def piece(j, h):
        return grad[pl.ds(pl.multiple_of((m ^ j) * 2 * half + (side ^ h) * half, half), half), :]

    for k, (j, h) in enumerate(((0, 0), (0, 1), (2, 0), (2, 1))):
        g_send[k * half:(k + 1) * half, :] = piece(j ^ 1, h)
        (g_0, g_1, g_2, g_3)[k][...] = piece(j, h)
    most = jnp.max(jnp.abs(grad[...]))
    loss = (jnp.sum(stats[0]) - (l_0 + l_1)) / width
    gsum = (jnp.sum(stats[1]) - 2 * rows) / width
    gscale = scale * (jnp.sum(stats[2]) - (s_0 + s_1)) / width
    row = lax.broadcasted_iota(jnp.int32, tail.shape, 0)
    values = jnp.zeros(tail.shape, F32)
    for k, v in enumerate((most, loss, gsum, gscale)):
        values = jnp.where(row == k, v, values)
    tail[...] = values
    g_send[4 * half:, :] = values


def call(kernel, outs, inputs, scratch, sems, limit=32):
    def spec(v):
        return SMEM if v.ndim == 1 else ANY

    return pl.pallas_call(
        kernel,
        out_shape=[jax.ShapeDtypeStruct(*o) for o in outs],
        in_specs=[spec(v) for v in inputs],
        out_specs=[VMEM] * len(outs),
        scratch_shapes=[pltpu.VMEM(*s) for s in scratch] + [pltpu.SemaphoreType.DMA((sems,))],
        compiler_params=pltpu.CompilerParams(vmem_limit_bytes=limit * 2**20),
        cost_estimate=pl.CostEstimate(flops=1, bytes_accessed=1, transcendentals=0),
    )(*inputs)


def encode(values, tail):
    return (values * (16384.0 / (tail[:1] + 1e-30))).astype(F16)


def decode(message, tail):
    return message.astype(F32) * ((tail[:1] + 1e-30) * (1.0 / 16384.0))


def top_row(v):
    return lax.broadcasted_iota(jnp.int32, v.shape, 0) == 0


def encode_with_tail(values, tail):
    power = jnp.ceil(jnp.log2(tail[:1] + 1e-30))
    tail = jnp.where(top_row(tail), power, tail * (1.0 / 64.0))
    high = lax.reduce_precision(tail, exponent_bits=5, mantissa_bits=10)
    return jnp.concatenate([values * jnp.exp2(14.0 - power), high, tail - high], axis=0).astype(F16)


def decode_tail(message):
    rows = message.shape[0] - 16
    tail = message[rows:rows + 8].astype(F32) + message[rows + 8:].astype(F32)
    return jnp.where(top_row(tail), jnp.exp2(tail), tail * 64.0)


def decode_with_tail(message):
    rows = message.shape[0] - 16
    power = message[rows:rows + 1].astype(F32)
    return message[:rows].astype(F32) * jnp.exp2(power - 14.0), decode_tail(message)


def per_device(n_batch, img_feat, txt_feat, img_proj, txt_proj, logit_scale, bias):
    rows, wide = img_feat.shape
    embed = img_proj.shape[1]
    n = n_batch * 4
    width = 8 * rows
    b = lax.axis_index("batch")
    m = lax.axis_index("mp")
    role, side, zh, c = b & 1, b >> 1 & 1, b >> 2 & 1, m & 1
    home = (c == zh).astype(jnp.int32)
    images = role == 0
    flags = jnp.stack([home, m, side])
    scal = jnp.stack([jnp.exp(logit_scale), bias])

    def send(v, home, away, name):
        with jax.named_scope(name):
            return lax.ppermute(v, AXES, pairs(n, home, away))

    def both(v, flip, name):
        return send(v, flip, flip, name)

    swap = ZH | C
    mine = jnp.where(images, img_feat, txt_feat)
    opp = jnp.where(images, txt_feat, img_feat)
    w0 = jnp.concatenate([jnp.where(images, img_proj, txt_proj), jnp.where(images, txt_proj, img_proj)], axis=0)
    p1 = send(mine, ROLE, swap, "mine_swap")
    w2 = both(w0, X, "proj_x")
    w1 = both(w0, C, "proj_core")
    s0 = send(opp, C, None, "sib_opp")
    p0 = send(opp, SIDE, None, "opp_home_side")
    w3 = both(w2, C, "proj_xcore")
    p1, w2, opp_late, p0 = lax.optimization_barrier((p1, w2, opp, p0))
    p2 = send(opp_late, ROLE, swap, "opp_swap")
    p3 = send(p1, SIDE, ROLE, "mine_square")
    s1 = send(p1, C, None, "sib_mine")

    square = (wide, embed)
    one, two = (rows, embed), (2 * rows, embed)
    norm = (rows, 128)
    stat = (3, 8, LANES)
    w_m, w_o, z_0, zf_0, r_0, acc_0, zo_a, stats = call(
        first_kernel,
        [(square, BF16), (square, BF16), (one, BF16), (one, F32), (norm, F32), (one, F32), (two, BF16), (stat, F32)],
        [flags, scal, w0, w1, w2, w3, mine, p1, opp, s0, p1, s1],
        [((4, *w0.shape), BF16), ((3 * rows, wide), BF16)],
        7,
    )
    p2, p3, w_o = lax.optimization_barrier((p2, p3, w_o))
    p6 = send(p2, None, ROLE, "opp_square_role")
    (zo_b,) = call(embed_kernel, [(two, BF16)], [flags, w_o, p3, p0, p2], [(square, BF16), (two, BF16)], 3)
    zo_c = both(zo_b, C, "sib_square")
    p4 = send(zo_b, None, SIDE, "square_side")
    acc_0, stats = call(
        next_kernel,
        [(one, F32), (stat, F32)],
        [flags, scal, z_0, acc_0, stats, zo_b, zo_c],
        [(one, BF16), ((4 * rows, embed), BF16)],
        5,
    )
    p6, acc_0, stats = lax.optimization_barrier((p6, acc_0, stats))
    z_1, zf_1, r_1, acc_1, stats = call(
        late_kernel,
        [(one, BF16), (one, F32), (norm, F32), (one, F32), (stat, F32)],
        [flags, scal, w_m, stats, zo_a, zo_b, zo_c, p2, p6],
        [(square, BF16), (one, BF16), ((6 * rows, embed), BF16)],
        6,
    )
    p4, acc_1 = lax.optimization_barrier((p4, acc_1))
    s4 = send(p4, None, C, "sib_side")
    half = wide // 8
    pieces, *kept, tail = call(
        functools.partial(last_kernel, width),
        [((4 * half + 8, embed), F32)] + [((half, embed), F32)] * 4 + [((8, embed), F32)],
        [flags, scal, z_0, z_1, zf_0, zf_1, r_0, r_1, acc_0, acc_1, stats, zo_a, zo_b, mine, p1, p2, p6, s4, p4],
        [
            (two, BF16), (two, BF16), (two, F32), ((2 * rows, 128), F32), (two, BF16), (two, BF16), (two, F32),
            (stat, F32), (square, F32),
        ],
        14,
    )

    got = both(pieces, C, "core_sum")
    tail = tail + got[4 * half:]
    kept = [v + got[k * half:(k + 1) * half] for k, v in enumerate(kept)]
    messages = lax.optimization_barrier(tuple(encode_with_tail(v, tail) for v in kept[1:]))
    ways = (SIDE, X, X | SIDE)
    came = lax.optimization_barrier(tuple(both(v, flip, "square_sum") for v, flip in zip(messages, ways)))
    parts = [decode_with_tail(v) for v in came]
    tails = [decode_tail(messages[0])] + [t for _, t in parts]
    total = (kept[0] + parts[0][0]) + (parts[1][0] + parts[2][0])
    tail = (tails[0] + tails[1]) + (tails[2] + tails[3])
    flip = ZH
    while flip < n:
        message, tail = lax.optimization_barrier((encode(total, tail), tail))
        other, more = lax.optimization_barrier((both(message, flip, "half_sum"), both(tail, flip, "half_sum")))
        total = decode(message, tail) + decode(other, more)
        tail = tail + more
        flip *= 2
    message, tail = lax.optimization_barrier((encode(total, tail), tail))
    by_s, by_r, by_rs, more = lax.optimization_barrier((
        both(message, SIDE, "hand_out"),
        both(message, ROLE, "hand_out"),
        both(message, ROLE | SIDE, "hand_out"),
        both(tail, ROLE, "hand_out"),
    ))

    def order(first, second, t):
        first, second = decode(first, t), decode(second, t)
        return jnp.concatenate([jnp.where(side == 0, first, second), jnp.where(side == 0, second, first)], axis=0)

    here, there = order(message, by_s, tail), order(by_r, by_rs, more)
    sums = jnp.where(images, tail, more)[:, 0] / (rows * n)
    return (sums[1], sums[3], sums[2], jnp.where(images, here, there), jnp.where(images, there, here))


def solution(mesh):
    return jax.shard_map(
        functools.partial(per_device, mesh.shape["batch"]),
        mesh=mesh,
        in_specs=(
            P(AXES, None),
            P(AXES, None),
            P("mp", None),
            P("mp", None),
            P(),
            P(),
        ),
        out_specs=(P(), P(), P(), P("mp", None), P("mp", None)),
        check_vma=False,
    )
```

```python
import functools

import jax
import jax.numpy as jnp
from jax import lax
from jax.experimental import pallas as pl
from jax.experimental.pallas import tpu as pltpu
from jax.sharding import PartitionSpec as P

AXES = ("batch", "mp")
LOG2E = 1.4426950408889634
STEP = 256
LANES = 512
F32 = jnp.float32
F16 = jnp.float16
BF16 = jnp.bfloat16
C, X, ROLE, SIDE, ZH = 1, 2, 4, 8, 16
ANY = pl.BlockSpec(memory_space=pl.ANY)
SMEM = pl.BlockSpec(memory_space=pltpu.SMEM)
VMEM = pl.BlockSpec(memory_space=pltpu.VMEM)


def is_home(i):
    b, m = divmod(i, 4)
    return m & 1 == b >> 2 & 1


def pairs(n, home, away):
    flips = [home if is_home(i) else away for i in range(n)]
    return [(i, i ^ f) for i, f in enumerate(flips) if f is not None]


def normalize(u):
    r = lax.rsqrt(jnp.sum(u * u, axis=1, keepdims=True) + 1e-06)
    return u * r, r


def project(feat, w):
    return normalize(jnp.dot(feat, w, preferred_element_type=F32))


def fold(v):
    v = jnp.sum(v.reshape(v.shape[0] // 8, 8, v.shape[1]), axis=0)
    return sum(v[:, k:k + LANES] for k in range(0, v.shape[1], LANES))


def fetch(flags, pair, dst, sem):
    if not isinstance(pair, tuple):
        copy = pltpu.make_async_copy(pair, dst, sem)
        copy.start()
        return copy
    first, second = (pltpu.make_async_copy(p, dst, sem) for p in pair)

    @pl.when(flags[0] == 1)
    def _():
        first.start()

    @pl.when(flags[0] != 1)
    def _():
        second.start()

    return first


def pair_terms(scal, z_m, lo, hi, zo, acc, stats):
    a = scal[0] * LOG2E
    b = scal[1] * LOG2E

    def sims(i):
        return lax.dot_general(z_m[i:i + STEP, :], zo, (((1,), (1,)), ((), ())), preferred_element_type=F32)

    s = sims(lo)
    for i in range(lo, hi, STEP):
        ahead = sims(i + STEP) if i + STEP < hi else None
        t = jnp.exp2(s * a + b)
        d = 1.0 + t
        sig = t * pltpu.reciprocal(d, approx=False)
        q = STEP // 4
        d4 = (d[:q] * d[q:2 * q]) * (d[2 * q:3 * q] * d[3 * q:])
        stats[0] += fold(jnp.log(d4))
        stats[1] += fold(sig)
        stats[2] += fold(sig * s)
        acc[i:i + STEP, :] += jnp.dot(sig.astype(BF16), zo, preferred_element_type=F32)
        s = ahead


def first_kernel(flags, scal, w0, w1, w2, w3, m_h, m_a, o0_h, o0_a, o1_h, o1_a,
                 w_m, w_o, z_m, zf, r_out, acc, z_o, stats, w_in, f_in, sems):
    rows = f_in.shape[0] // 3
    part = w0.shape[0] // 2
    m = flags[1]
    copies = [fetch(flags, w, w_in.at[j], sems.at[j]) for j, w in enumerate((w0, w1, w2, w3))]
    copies += [
        fetch(flags, p, f_in.at[pl.ds(k * rows, rows), :], sems.at[4 + k])
        for k, p in enumerate(((m_h, m_a), (o0_h, o0_a), (o1_h, o1_a)))
    ]
    acc[...] = jnp.zeros_like(acc)
    stats[...] = jnp.zeros_like(stats)
    for j in range(4):
        copies[j].wait()
        at = pl.multiple_of((m ^ j) * part, part)
        w_m[pl.ds(at, part), :] = w_in[j, :part, :]
        w_o[pl.ds(at, part), :] = w_in[j, part:, :]
    copies[4].wait()
    zf_m, r = project(f_in[:rows, :], w_m[...])
    zf[...] = zf_m
    r_out[...] = jnp.broadcast_to(r, r_out.shape)
    z_m[...] = zf_m.astype(BF16)
    for k in range(2):
        copies[5 + k].wait()
        z_o[k * rows:(k + 1) * rows, :] = project(f_in[(k + 1) * rows:(k + 2) * rows, :], w_o[...])[0].astype(BF16)
    pair_terms(scal, z_m, 0, rows, z_o[...], acc, stats)


def embed_kernel(flags, w_o, o0, o1_h, o1_a, z_o, f_in, sems):
    rows = f_in.shape[0] // 2
    copies = [fetch(flags, p, f_in.at[pl.ds(k * rows, rows), :], sems.at[k]) for k, p in enumerate((o0, (o1_h, o1_a)))]
    for k in range(2):
        copies[k].wait()
        z_o[k * rows:(k + 1) * rows, :] = project(f_in[k * rows:(k + 1) * rows, :], w_o[...])[0].astype(BF16)


def next_kernel(flags, scal, z_m, acc_in, stats_in, own, sibling, acc, stats, z_in, z_o, sems):
    rows = z_in.shape[0]
    copies = [
        fetch(flags, z_m, z_in, sems.at[0]),
        fetch(flags, own, z_o.at[pl.ds(0, 2 * rows), :], sems.at[1]),
        fetch(flags, sibling, z_o.at[pl.ds(2 * rows, 2 * rows), :], sems.at[2]),
        fetch(flags, acc_in, acc, sems.at[3]),
        fetch(flags, stats_in, stats, sems.at[4]),
    ]
    for c in copies:
        c.wait()
    pair_terms(scal, z_in, 0, rows, z_o[...], acc, stats)


def late_kernel(flags, scal, w_m, stats_in, zo_a, zo_b, zo_c, m1_h, m1_a, z_m, zf, r_out, acc, stats, f_in, z_o, sems):
    rows = f_in.shape[0]
    copies = [
        fetch(flags, (m1_h, m1_a), f_in, sems.at[0]),
        fetch(flags, stats_in, stats, sems.at[1]),
    ]
    copies += [fetch(flags, v, z_o.at[pl.ds(2 * k * rows, 2 * rows), :], sems.at[2 + k]) for k, v in enumerate((zo_a, zo_b, zo_c))]
    acc[...] = jnp.zeros_like(acc)
    copies[0].wait()
    zf_m, r = project(f_in[...], w_m[...])
    zf[...] = zf_m
    r_out[...] = jnp.broadcast_to(r, r_out.shape)
    z_m[...] = zf_m.astype(BF16)
    for c in copies[1:]:
        c.wait()
    pair_terms(scal, z_m, 0, rows, z_o[:3 * rows, :], acc, stats)
    pair_terms(scal, z_m, 0, rows, z_o[3 * rows:, :], acc, stats)


def last_kernel(width, flags, scal, z_0, z_1, zf_0, zf_1, r_0, r_1, acc_0, acc_1, stats_in, zo_a, zo_b,
                m0_h, m0_a, m1_h, m1_a, o_h, o_a,
                g_send, g_0, g_1, g_2, g_3, tail, feat, z, zf, r, z_o, z_own, acc, stats, grad, sems):
    rows = r.shape[0] // 2
    home, m, side = flags[0], flags[1], flags[2]
    scale, bias = scal[0], scal[1]

    def span(k):
        return pl.ds(k * rows, rows)

    def get(k, src, dst):
        return fetch(flags, src, dst, sems.at[k])

    now = [get(k, v, z.at[span(k), :]) for k, v in enumerate((z_0, z_1))]
    now += [get(2, (o_h, o_a), z_o), get(3, stats_in, stats)]
    now += [get(4 + k, v, acc.at[span(k), :]) for k, v in enumerate((acc_0, acc_1))]
    rest = [get(6 + k, v, zf.at[span(k), :]) for k, v in enumerate((zf_0, zf_1))]
    rest += [get(8 + k, v, r.at[span(k), :]) for k, v in enumerate((r_0, r_1))]
    rest += [get(10 + k, v, feat.at[span(k), :]) for k, v in enumerate(((m0_h, m0_a), (m1_h, m1_a)))]
    first = (zo_a.at[span(0), :], zo_b.at[span(1), :])
    second = (zo_a.at[span(1), :], zo_b.at[span(0), :])
    rest += [get(12 + k, v, z_own.at[span(k), :]) for k, v in enumerate((first, second))]
    for c in now:
        c.wait()
    pair_terms(scal, z, 0, 2 * rows, z_o[...], acc, stats)
    for c in rest:
        c.wait()

    def finish(k):
        at = slice(k * rows, (k + 1) * rows)
        pair = z_own[at, :].astype(F32)
        s = jnp.sum(z[at, :].astype(F32) * pair, axis=1, keepdims=True)
        l = scale * s + bias
        t = jnp.exp2(s * (scale * LOG2E) + bias * LOG2E)
        rest = pltpu.reciprocal(1.0 + t, approx=False)
        change = (-rest).astype(BF16).astype(F32) - (t * rest).astype(BF16).astype(F32)
        dz = (scale / width) * (acc[at, :] + change * pair)
        zf_k = zf[at, :]
        du = (r[at, :1] * (dz - zf_k * jnp.sum(zf_k * dz, axis=1, keepdims=True))).astype(BF16)
        return du, jnp.sum(s), jnp.sum(l)

    def gradient(k, du):
        return lax.dot_general(feat[k * rows:(k + 1) * rows, :], du, (((0,), (0,)), ((), ())), preferred_element_type=F32)

    du_0, s_0, l_0 = finish(0)
    part_0 = gradient(0, du_0)
    du_1, s_1, l_1 = finish(1)
    grad[...] = part_0 + gradient(1, du_1)
    half = grad.shape[0] // 8

    def piece(j, h):
        return grad[pl.ds(pl.multiple_of((m ^ j) * 2 * half + (side ^ h) * half, half), half), :]

    for k, (j, h) in enumerate(((0, 0), (0, 1), (2, 0), (2, 1))):
        g_send[k * half:(k + 1) * half, :] = piece(j ^ 1, h)
        (g_0, g_1, g_2, g_3)[k][...] = piece(j, h)
    most = jnp.max(jnp.abs(grad[...]))
    loss = (jnp.sum(stats[0]) - (l_0 + l_1)) / width
    gsum = (jnp.sum(stats[1]) - 2 * rows) / width
    gscale = scale * (jnp.sum(stats[2]) - (s_0 + s_1)) / width
    row = lax.broadcasted_iota(jnp.int32, tail.shape, 0)
    values = jnp.zeros(tail.shape, F32)
    for k, v in enumerate((most, loss, gsum, gscale)):
        values = jnp.where(row == k, v, values)
    tail[...] = values
    g_send[4 * half:, :] = values


def call(kernel, outs, inputs, scratch, sems, resident=(), limit=32):
    def spec(k, v):
        return SMEM if v.ndim == 1 else VMEM if k in resident else ANY

    return pl.pallas_call(
        kernel,
        out_shape=[jax.ShapeDtypeStruct(*o) for o in outs],
        in_specs=[spec(k, v) for k, v in enumerate(inputs)],
        out_specs=[VMEM] * len(outs),
        scratch_shapes=[pltpu.VMEM(*s) for s in scratch] + [pltpu.SemaphoreType.DMA((sems,))],
        compiler_params=pltpu.CompilerParams(vmem_limit_bytes=limit * 2**20),
        cost_estimate=pl.CostEstimate(flops=1, bytes_accessed=1, transcendentals=0),
    )(*inputs)


def encode(values, tail):
    return (values * (16384.0 / (tail[:1] + 1e-30))).astype(F16)


def decode(message, tail):
    return message.astype(F32) * ((tail[:1] + 1e-30) * (1.0 / 16384.0))


def top_row(v):
    return lax.broadcasted_iota(jnp.int32, v.shape, 0) == 0


def encode_with_tail(values, tail):
    power = jnp.ceil(jnp.log2(tail[:1] + 1e-30))
    tail = jnp.where(top_row(tail), power, tail * (1.0 / 64.0))
    high = lax.reduce_precision(tail, exponent_bits=5, mantissa_bits=10)
    return jnp.concatenate([values * jnp.exp2(14.0 - power), high, tail - high], axis=0).astype(F16)


def decode_tail(message):
    rows = message.shape[0] - 16
    tail = message[rows:rows + 8].astype(F32) + message[rows + 8:].astype(F32)
    return jnp.where(top_row(tail), jnp.exp2(tail), tail * 64.0)


def decode_with_tail(message):
    rows = message.shape[0] - 16
    power = message[rows:rows + 1].astype(F32)
    return message[:rows].astype(F32) * jnp.exp2(power - 14.0), decode_tail(message)


def per_device(n_batch, img_feat, txt_feat, img_proj, txt_proj, logit_scale, bias):
    rows, wide = img_feat.shape
    embed = img_proj.shape[1]
    n = n_batch * 4
    width = 8 * rows
    b = lax.axis_index("batch")
    m = lax.axis_index("mp")
    role, side, zh, c = b & 1, b >> 1 & 1, b >> 2 & 1, m & 1
    home = (c == zh).astype(jnp.int32)
    images = role == 0
    flags = jnp.stack([home, m, side])
    scal = jnp.stack([jnp.exp(logit_scale), bias])

    def send(v, home, away, name):
        with jax.named_scope(name):
            return lax.ppermute(v, AXES, pairs(n, home, away))

    def both(v, flip, name):
        return send(v, flip, flip, name)

    swap = ZH | C
    mine = jnp.where(images, img_feat, txt_feat)
    opp = jnp.where(images, txt_feat, img_feat)
    w0 = jnp.concatenate([jnp.where(images, img_proj, txt_proj), jnp.where(images, txt_proj, img_proj)], axis=0)
    p1 = send(mine, ROLE, swap, "mine_swap")
    w2 = both(w0, X, "proj_x")
    w1 = both(w0, C, "proj_core")
    s0 = send(opp, C, None, "sib_opp")
    p0 = send(opp, SIDE, None, "opp_home_side")
    w3 = both(w2, C, "proj_xcore")
    w2, p0 = lax.optimization_barrier((w2, p0))
    p1, w2, opp_late = lax.optimization_barrier((p1, w2, opp))
    p2 = send(opp_late, ROLE, swap, "opp_swap")
    p3 = send(p1, SIDE, ROLE, "mine_square")
    s1 = send(p1, C, None, "sib_mine")

    square = (wide, embed)
    one, two = (rows, embed), (2 * rows, embed)
    norm = (rows, 128)
    stat = (3, 8, LANES)
    w_m, w_o, z_0, zf_0, r_0, acc_0, zo_a, stats = call(
        first_kernel,
        [(square, BF16), (square, BF16), (one, BF16), (one, F32), (norm, F32), (one, F32), (two, BF16), (stat, F32)],
        [flags, scal, w0, w1, w2, w3, mine, p1, opp, s0, p1, s1],
        [((4, *w0.shape), BF16), ((3 * rows, wide), BF16)],
        7,
    )
    p2, p3, w_o = lax.optimization_barrier((p2, p3, w_o))
    p6 = send(p2, None, ROLE, "opp_square_role")
    (zo_b,) = call(embed_kernel, [(two, BF16)], [flags, w_o, p3, p0, p2], [(two, BF16)], 2, (1,))
    zo_c = both(zo_b, C, "sib_square")
    p4 = send(zo_b, None, SIDE, "square_side")
    acc_0, stats = call(
        next_kernel,
        [(one, F32), (stat, F32)],
        [flags, scal, z_0, acc_0, stats, zo_b, zo_c],
        [(one, BF16), ((4 * rows, embed), BF16)],
        5,
    )
    p6, acc_0, stats = lax.optimization_barrier((p6, acc_0, stats))
    z_1, zf_1, r_1, acc_1, stats = call(
        late_kernel,
        [(one, BF16), (one, F32), (norm, F32), (one, F32), (stat, F32)],
        [flags, scal, w_m, stats, zo_a, zo_b, zo_c, p2, p6],
        [(one, BF16), ((6 * rows, embed), BF16)],
        5,
        (2,),
    )
    p4, acc_1 = lax.optimization_barrier((p4, acc_1))
    s4 = send(p4, None, C, "sib_side")
    half = wide // 8
    pieces, *kept, tail = call(
        functools.partial(last_kernel, width),
        [((4 * half + 8, embed), F32)] + [((half, embed), F32)] * 4 + [((8, embed), F32)],
        [flags, scal, z_0, z_1, zf_0, zf_1, r_0, r_1, acc_0, acc_1, stats, zo_a, zo_b, mine, p1, p2, p6, s4, p4],
        [
            (two, BF16), (two, BF16), (two, F32), ((2 * rows, 128), F32), (two, BF16), (two, BF16), (two, F32),
            (stat, F32), (square, F32),
        ],
        14,
    )

    got = both(pieces, C, "core_sum")
    tail = tail + got[4 * half:]
    kept = [v + got[k * half:(k + 1) * half] for k, v in enumerate(kept)]
    messages = lax.optimization_barrier(tuple(encode_with_tail(v, tail) for v in kept[1:]))
    ways = (SIDE, X, X | SIDE)
    came = lax.optimization_barrier(tuple(both(v, flip, "square_sum") for v, flip in zip(messages, ways)))
    parts = [decode_with_tail(v) for v in came]
    tails = [decode_tail(messages[0])] + [t for _, t in parts]
    total = (kept[0] + parts[0][0]) + (parts[1][0] + parts[2][0])
    tail = (tails[0] + tails[1]) + (tails[2] + tails[3])
    flip = ZH
    while flip < n:
        message, tail = lax.optimization_barrier((encode(total, tail), tail))
        other, more = lax.optimization_barrier((both(message, flip, "half_sum"), both(tail, flip, "half_sum")))
        total = decode(message, tail) + decode(other, more)
        tail = tail + more
        flip *= 2
    message, tail = lax.optimization_barrier((encode(total, tail), tail))
    by_s, by_r, by_rs, more = lax.optimization_barrier((
        both(message, SIDE, "hand_out"),
        both(message, ROLE, "hand_out"),
        both(message, ROLE | SIDE, "hand_out"),
        both(tail, ROLE, "hand_out"),
    ))

    def order(first, second, t):
        first, second = decode(first, t), decode(second, t)
        return jnp.concatenate([jnp.where(side == 0, first, second), jnp.where(side == 0, second, first)], axis=0)

    here, there = order(message, by_s, tail), order(by_r, by_rs, more)
    sums = jnp.where(images, tail, more)[:, 0] / (rows * n)
    return (sums[1], sums[3], sums[2], jnp.where(images, here, there), jnp.where(images, there, here))


def solution(mesh):
    return jax.shard_map(
        functools.partial(per_device, mesh.shape["batch"]),
        mesh=mesh,
        in_specs=(
            P(AXES, None),
            P(AXES, None),
            P("mp", None),
            P("mp", None),
            P(),
            P(),
        ),
        out_specs=(P(), P(), P(), P("mp", None), P("mp", None)),
        check_vma=False,
    )
```

```python
import functools

import jax
import jax.numpy as jnp
from jax import lax
from jax.experimental import pallas as pl
from jax.experimental.pallas import tpu as pltpu
from jax.sharding import PartitionSpec as P

AXES = ("batch", "mp")
LOG2E = 1.4426950408889634
STEP = 256
LANES = 512
F32 = jnp.float32
F16 = jnp.float16
BF16 = jnp.bfloat16
C, X, ROLE, SIDE, ZH = 1, 2, 4, 8, 16
ANY = pl.BlockSpec(memory_space=pl.ANY)
SMEM = pl.BlockSpec(memory_space=pltpu.SMEM)
VMEM = pl.BlockSpec(memory_space=pltpu.VMEM)


def is_home(i):
    b, m = divmod(i, 4)
    return m & 1 == b >> 2 & 1


def pairs(n, home, away):
    flips = [home if is_home(i) else away for i in range(n)]
    return [(i, i ^ f) for i, f in enumerate(flips) if f is not None]


def normalize(u):
    r = lax.rsqrt(jnp.sum(u * u, axis=1, keepdims=True) + 1e-06)
    return u * r, r


def project(feat, w):
    return normalize(jnp.dot(feat, w, preferred_element_type=F32))


def fold(v):
    v = jnp.sum(v.reshape(v.shape[0] // 8, 8, v.shape[1]), axis=0)
    return sum(v[:, k:k + LANES] for k in range(0, v.shape[1], LANES))


def fetch(flags, pair, dst, sem):
    if not isinstance(pair, tuple):
        copy = pltpu.make_async_copy(pair, dst, sem)
        copy.start()
        return copy
    first, second = (pltpu.make_async_copy(p, dst, sem) for p in pair)

    @pl.when(flags[0] == 1)
    def _():
        first.start()

    @pl.when(flags[0] != 1)
    def _():
        second.start()

    return first


def pair_terms(scal, z_m, lo, hi, zo, acc, stats):
    a = scal[0] * LOG2E
    b = scal[1] * LOG2E

    def sims(i):
        return lax.dot_general(z_m[i:i + STEP, :], zo, (((1,), (1,)), ((), ())), preferred_element_type=F32)

    s = sims(lo)
    for i in range(lo, hi, STEP):
        ahead = sims(i + STEP) if i + STEP < hi else None
        t = jnp.exp2(s * a + b)
        d = 1.0 + t
        sig = t * pltpu.reciprocal(d, approx=False)
        q = STEP // 4
        d4 = (d[:q] * d[q:2 * q]) * (d[2 * q:3 * q] * d[3 * q:])
        stats[0] += fold(jnp.log(d4))
        stats[1] += fold(sig)
        stats[2] += fold(sig * s)
        acc[i:i + STEP, :] += jnp.dot(sig.astype(BF16), zo, preferred_element_type=F32)
        s = ahead


def first_kernel(flags, scal, w0, w1, w2, w3, m_h, m_a, o0_h, o0_a, o1_h, o1_a,
                 w_m, w_o, z_m, zf, r_out, acc, z_o, stats, w_in, f_in, sems):
    rows = f_in.shape[0] // 3
    part = w0.shape[0] // 2
    m = flags[1]
    copies = [fetch(flags, w, w_in.at[j], sems.at[j]) for j, w in enumerate((w0, w1, w2, w3))]
    copies += [
        fetch(flags, p, f_in.at[pl.ds(k * rows, rows), :], sems.at[4 + k])
        for k, p in enumerate(((m_h, m_a), (o0_h, o0_a), (o1_h, o1_a)))
    ]
    acc[...] = jnp.zeros_like(acc)
    stats[...] = jnp.zeros_like(stats)
    for j in range(4):
        copies[j].wait()
        at = pl.multiple_of((m ^ j) * part, part)
        w_m[pl.ds(at, part), :] = w_in[j, :part, :]
        w_o[pl.ds(at, part), :] = w_in[j, part:, :]
    copies[4].wait()
    zf_m, r = project(f_in[:rows, :], w_m[...])
    zf[...] = zf_m
    r_out[...] = jnp.broadcast_to(r, r_out.shape)
    z_m[...] = zf_m.astype(BF16)
    for k in range(2):
        copies[5 + k].wait()
        z_o[k * rows:(k + 1) * rows, :] = project(f_in[(k + 1) * rows:(k + 2) * rows, :], w_o[...])[0].astype(BF16)
    pair_terms(scal, z_m, 0, rows, z_o[...], acc, stats)


def embed_kernel(flags, w_o, o0, o1_h, o1_a, z_o, f_in, sems):
    rows = f_in.shape[0] // 2
    copies = [fetch(flags, p, f_in.at[pl.ds(k * rows, rows), :], sems.at[k]) for k, p in enumerate((o0, (o1_h, o1_a)))]
    for k in range(2):
        copies[k].wait()
        z_o[k * rows:(k + 1) * rows, :] = project(f_in[k * rows:(k + 1) * rows, :], w_o[...])[0].astype(BF16)


def next_kernel(flags, scal, z_m, acc_in, stats_in, own, sibling, acc, stats, z_in, z_o, sems):
    rows = z_in.shape[0]
    copies = [
        fetch(flags, z_m, z_in, sems.at[0]),
        fetch(flags, own, z_o.at[pl.ds(0, 2 * rows), :], sems.at[1]),
        fetch(flags, sibling, z_o.at[pl.ds(2 * rows, 2 * rows), :], sems.at[2]),
        fetch(flags, acc_in, acc, sems.at[3]),
        fetch(flags, stats_in, stats, sems.at[4]),
    ]
    for c in copies:
        c.wait()
    pair_terms(scal, z_in, 0, rows, z_o[...], acc, stats)


def late_kernel(flags, scal, w_m, stats_in, zo_a, zo_b, m1_h, m1_a, z_m, zf, r_out, acc, stats, f_in, z_o, sems):
    rows = f_in.shape[0]
    copies = [
        fetch(flags, (m1_h, m1_a), f_in, sems.at[0]),
        fetch(flags, stats_in, stats, sems.at[1]),
    ]
    copies += [fetch(flags, v, z_o.at[pl.ds(2 * k * rows, 2 * rows), :], sems.at[2 + k]) for k, v in enumerate((zo_a, zo_b))]
    acc[...] = jnp.zeros_like(acc)
    copies[0].wait()
    zf_m, r = project(f_in[...], w_m[...])
    zf[...] = zf_m
    r_out[...] = jnp.broadcast_to(r, r_out.shape)
    z_m[...] = zf_m.astype(BF16)
    for c in copies[1:]:
        c.wait()
    pair_terms(scal, z_m, 0, rows, z_o[...], acc, stats)


def rest_kernel(flags, scal, z_m, acc_in, stats_in, others, acc, stats, z_in, z_o, sems):
    rows = z_in.shape[0]
    pairs_of = ((z_m, z_in), (others, z_o), (acc_in, acc), (stats_in, stats))
    copies = [fetch(flags, src, dst, sems.at[k]) for k, (src, dst) in enumerate(pairs_of)]
    for c in copies:
        c.wait()
    pair_terms(scal, z_in, 0, rows, z_o[...], acc, stats)


def last_kernel(width, flags, scal, z_0, z_1, zf_0, zf_1, r_0, r_1, acc_0, acc_1, stats_in, zo_a, zo_b,
                m0_h, m0_a, m1_h, m1_a, o_h, o_a,
                g_send, g_0, g_1, g_2, g_3, tail, feat, z, zf, r, z_o, z_own, acc, stats, grad, sems):
    rows = r.shape[0] // 2
    home, m, side = flags[0], flags[1], flags[2]
    scale, bias = scal[0], scal[1]

    def span(k):
        return pl.ds(k * rows, rows)

    def get(k, src, dst):
        return fetch(flags, src, dst, sems.at[k])

    now = [get(k, v, z.at[span(k), :]) for k, v in enumerate((z_0, z_1))]
    now += [get(2, (o_h, o_a), z_o), get(3, stats_in, stats)]
    now += [get(4 + k, v, acc.at[span(k), :]) for k, v in enumerate((acc_0, acc_1))]
    rest = [get(6 + k, v, zf.at[span(k), :]) for k, v in enumerate((zf_0, zf_1))]
    rest += [get(8 + k, v, r.at[span(k), :]) for k, v in enumerate((r_0, r_1))]
    rest += [get(10 + k, v, feat.at[span(k), :]) for k, v in enumerate(((m0_h, m0_a), (m1_h, m1_a)))]
    first = (zo_a.at[span(0), :], zo_b.at[span(1), :])
    second = (zo_a.at[span(1), :], zo_b.at[span(0), :])
    rest += [get(12 + k, v, z_own.at[span(k), :]) for k, v in enumerate((first, second))]
    for c in now:
        c.wait()
    pair_terms(scal, z, 0, 2 * rows, z_o[...], acc, stats)
    for c in rest:
        c.wait()

    def finish(k):
        at = slice(k * rows, (k + 1) * rows)
        pair = z_own[at, :].astype(F32)
        s = jnp.sum(z[at, :].astype(F32) * pair, axis=1, keepdims=True)
        l = scale * s + bias
        t = jnp.exp2(s * (scale * LOG2E) + bias * LOG2E)
        rest = pltpu.reciprocal(1.0 + t, approx=False)
        change = (-rest).astype(BF16).astype(F32) - (t * rest).astype(BF16).astype(F32)
        dz = (scale / width) * (acc[at, :] + change * pair)
        zf_k = zf[at, :]
        du = (r[at, :1] * (dz - zf_k * jnp.sum(zf_k * dz, axis=1, keepdims=True))).astype(BF16)
        return du, jnp.sum(s), jnp.sum(l)

    def gradient(k, du):
        return lax.dot_general(feat[k * rows:(k + 1) * rows, :], du, (((0,), (0,)), ((), ())), preferred_element_type=F32)

    du_0, s_0, l_0 = finish(0)
    part_0 = gradient(0, du_0)
    du_1, s_1, l_1 = finish(1)
    grad[...] = part_0 + gradient(1, du_1)
    half = grad.shape[0] // 8

    def piece(j, h):
        return grad[pl.ds(pl.multiple_of((m ^ j) * 2 * half + (side ^ h) * half, half), half), :]

    for k, (j, h) in enumerate(((0, 0), (0, 1), (2, 0), (2, 1))):
        g_send[k * half:(k + 1) * half, :] = piece(j ^ 1, h)
        (g_0, g_1, g_2, g_3)[k][...] = piece(j, h)
    most = jnp.max(jnp.abs(grad[...]))
    loss = (jnp.sum(stats[0]) - (l_0 + l_1)) / width
    gsum = (jnp.sum(stats[1]) - 2 * rows) / width
    gscale = scale * (jnp.sum(stats[2]) - (s_0 + s_1)) / width
    row = lax.broadcasted_iota(jnp.int32, tail.shape, 0)
    values = jnp.zeros(tail.shape, F32)
    for k, v in enumerate((most, loss, gsum, gscale)):
        values = jnp.where(row == k, v, values)
    tail[...] = values
    g_send[4 * half:, :] = values


def call(kernel, outs, inputs, scratch, sems, resident=(), limit=32):
    def spec(k, v):
        return SMEM if v.ndim == 1 else VMEM if k in resident else ANY

    return pl.pallas_call(
        kernel,
        out_shape=[jax.ShapeDtypeStruct(*o) for o in outs],
        in_specs=[spec(k, v) for k, v in enumerate(inputs)],
        out_specs=[VMEM] * len(outs),
        scratch_shapes=[pltpu.VMEM(*s) for s in scratch] + [pltpu.SemaphoreType.DMA((sems,))],
        compiler_params=pltpu.CompilerParams(vmem_limit_bytes=limit * 2**20),
        cost_estimate=pl.CostEstimate(flops=1, bytes_accessed=1, transcendentals=0),
    )(*inputs)


def encode(values, tail):
    return (values * (16384.0 / (tail[:1] + 1e-30))).astype(F16)


def decode(message, tail):
    return message.astype(F32) * ((tail[:1] + 1e-30) * (1.0 / 16384.0))


def top_row(v):
    return lax.broadcasted_iota(jnp.int32, v.shape, 0) == 0


def encode_with_tail(values, tail):
    power = jnp.ceil(jnp.log2(tail[:1] + 1e-30))
    tail = jnp.where(top_row(tail), power, tail * (1.0 / 64.0))
    high = lax.reduce_precision(tail, exponent_bits=5, mantissa_bits=10)
    return jnp.concatenate([values * jnp.exp2(14.0 - power), high, tail - high], axis=0).astype(F16)


def decode_tail(message):
    rows = message.shape[0] - 16
    tail = message[rows:rows + 8].astype(F32) + message[rows + 8:].astype(F32)
    return jnp.where(top_row(tail), jnp.exp2(tail), tail * 64.0)


def decode_with_tail(message):
    rows = message.shape[0] - 16
    power = message[rows:rows + 1].astype(F32)
    return message[:rows].astype(F32) * jnp.exp2(power - 14.0), decode_tail(message)


def per_device(n_batch, img_feat, txt_feat, img_proj, txt_proj, logit_scale, bias):
    rows, wide = img_feat.shape
    embed = img_proj.shape[1]
    n = n_batch * 4
    width = 8 * rows
    b = lax.axis_index("batch")
    m = lax.axis_index("mp")
    role, side, zh, c = b & 1, b >> 1 & 1, b >> 2 & 1, m & 1
    home = (c == zh).astype(jnp.int32)
    images = role == 0
    flags = jnp.stack([home, m, side])
    scal = jnp.stack([jnp.exp(logit_scale), bias])

    def send(v, home, away, name):
        with jax.named_scope(name):
            return lax.ppermute(v, AXES, pairs(n, home, away))

    def both(v, flip, name):
        return send(v, flip, flip, name)

    swap = ZH | C
    mine = jnp.where(images, img_feat, txt_feat)
    opp = jnp.where(images, txt_feat, img_feat)
    w0 = jnp.concatenate([jnp.where(images, img_proj, txt_proj), jnp.where(images, txt_proj, img_proj)], axis=0)
    p1 = send(mine, ROLE, swap, "mine_swap")
    w2 = both(w0, X, "proj_x")
    w1 = both(w0, C, "proj_core")
    s0 = send(opp, C, None, "sib_opp")
    p0 = send(opp, SIDE, None, "opp_home_side")
    w3 = both(w2, C, "proj_xcore")
    w2, p0 = lax.optimization_barrier((w2, p0))
    p1, w2, opp_late = lax.optimization_barrier((p1, w2, opp))
    p2 = send(opp_late, ROLE, swap, "opp_swap")
    p3 = send(p1, SIDE, ROLE, "mine_square")
    s1 = send(p1, C, None, "sib_mine")

    square = (wide, embed)
    one, two = (rows, embed), (2 * rows, embed)
    norm = (rows, 128)
    stat = (3, 8, LANES)
    w_m, w_o, z_0, zf_0, r_0, acc_0, zo_a, stats = call(
        first_kernel,
        [(square, BF16), (square, BF16), (one, BF16), (one, F32), (norm, F32), (one, F32), (two, BF16), (stat, F32)],
        [flags, scal, w0, w1, w2, w3, mine, p1, opp, s0, p1, s1],
        [((4, *w0.shape), BF16), ((3 * rows, wide), BF16)],
        7,
    )
    p2, p3, w_o = lax.optimization_barrier((p2, p3, w_o))
    p6 = send(p2, None, ROLE, "opp_square_role")
    (zo_b,) = call(embed_kernel, [(two, BF16)], [flags, w_o, p3, p0, p2], [(two, BF16)], 2, (1,))
    zo_c = both(zo_b, C, "sib_square")
    p4 = send(zo_b, None, SIDE, "square_side")
    acc_0, stats = call(
        next_kernel,
        [(one, F32), (stat, F32)],
        [flags, scal, z_0, acc_0, stats, zo_b, zo_c],
        [(one, BF16), ((4 * rows, embed), BF16)],
        5,
    )
    p6, acc_0, stats = lax.optimization_barrier((p6, acc_0, stats))
    z_1, zf_1, r_1, acc_1, stats = call(
        late_kernel,
        [(one, BF16), (one, F32), (norm, F32), (one, F32), (stat, F32)],
        [flags, scal, w_m, stats, zo_a, zo_b, p2, p6],
        [(one, BF16), ((4 * rows, embed), BF16)],
        4,
        (2,),
    )
    p4, acc_1 = lax.optimization_barrier((p4, acc_1))
    s4 = send(p4, None, C, "sib_side")
    acc_1, stats = call(
        rest_kernel,
        [(one, F32), (stat, F32)],
        [flags, scal, z_1, acc_1, stats, zo_c],
        [(one, BF16), (two, BF16)],
        4,
    )
    half = wide // 8
    pieces, *kept, tail = call(
        functools.partial(last_kernel, width),
        [((4 * half + 8, embed), F32)] + [((half, embed), F32)] * 4 + [((8, embed), F32)],
        [flags, scal, z_0, z_1, zf_0, zf_1, r_0, r_1, acc_0, acc_1, stats, zo_a, zo_b, mine, p1, p2, p6, s4, p4],
        [
            (two, BF16), (two, BF16), (two, F32), ((2 * rows, 128), F32), (two, BF16), (two, BF16), (two, F32),
            (stat, F32), (square, F32),
        ],
        14,
    )

    got = both(pieces, C, "core_sum")
    tail = tail + got[4 * half:]
    kept = [v + got[k * half:(k + 1) * half] for k, v in enumerate(kept)]
    messages = lax.optimization_barrier(tuple(encode_with_tail(v, tail) for v in kept[1:]))
    ways = (SIDE, X, X | SIDE)
    came = lax.optimization_barrier(tuple(both(v, flip, "square_sum") for v, flip in zip(messages, ways)))
    parts = [decode_with_tail(v) for v in came]
    tails = [decode_tail(messages[0])] + [t for _, t in parts]
    total = (kept[0] + parts[0][0]) + (parts[1][0] + parts[2][0])
    tail = (tails[0] + tails[1]) + (tails[2] + tails[3])
    flip = ZH
    while flip < n:
        message, tail = lax.optimization_barrier((encode(total, tail), tail))
        other, more = lax.optimization_barrier((both(message, flip, "half_sum"), both(tail, flip, "half_sum")))
        total = decode(message, tail) + decode(other, more)
        tail = tail + more
        flip *= 2
    message, tail = lax.optimization_barrier((encode(total, tail), tail))
    by_s, by_r, by_rs, more = lax.optimization_barrier((
        both(message, SIDE, "hand_out"),
        both(message, ROLE, "hand_out"),
        both(message, ROLE | SIDE, "hand_out"),
        both(tail, ROLE, "hand_out"),
    ))

    def order(first, second, t):
        first, second = decode(first, t), decode(second, t)
        return jnp.concatenate([jnp.where(side == 0, first, second), jnp.where(side == 0, second, first)], axis=0)

    here, there = order(message, by_s, tail), order(by_r, by_rs, more)
    sums = jnp.where(images, tail, more)[:, 0] / (rows * n)
    return (sums[1], sums[3], sums[2], jnp.where(images, here, there), jnp.where(images, there, here))


def solution(mesh):
    return jax.shard_map(
        functools.partial(per_device, mesh.shape["batch"]),
        mesh=mesh,
        in_specs=(
            P(AXES, None),
            P(AXES, None),
            P("mp", None),
            P("mp", None),
            P(),
            P(),
        ),
        out_specs=(P(), P(), P(), P("mp", None), P("mp", None)),
        check_vma=False,
    )
```

```python
import functools

import jax
import jax.numpy as jnp
from jax import lax
from jax.experimental import pallas as pl
from jax.experimental.pallas import tpu as pltpu
from jax.sharding import PartitionSpec as P

AXES = ("batch", "mp")
LOG2E = 1.4426950408889634
STEP = 256
LANES = 512
F32 = jnp.float32
F16 = jnp.float16
BF16 = jnp.bfloat16
C, X, ROLE, SIDE, ZH = 1, 2, 4, 8, 16
ANY = pl.BlockSpec(memory_space=pl.ANY)
SMEM = pl.BlockSpec(memory_space=pltpu.SMEM)
VMEM = pl.BlockSpec(memory_space=pltpu.VMEM)


def is_home(i):
    b, m = divmod(i, 4)
    return m & 1 == b >> 2 & 1


def pairs(n, home, away):
    flips = [home if is_home(i) else away for i in range(n)]
    return [(i, i ^ f) for i, f in enumerate(flips) if f is not None]


def normalize(u):
    r = lax.rsqrt(jnp.sum(u * u, axis=1, keepdims=True) + 1e-06)
    return u * r, r


def project(feat, w):
    return normalize(jnp.dot(feat, w, preferred_element_type=F32))


def fold(v):
    v = jnp.sum(v.reshape(v.shape[0] // 8, 8, v.shape[1]), axis=0)
    return sum(v[:, k:k + LANES] for k in range(0, v.shape[1], LANES))


def fetch(flags, pair, dst, sem):
    if not isinstance(pair, tuple):
        copy = pltpu.make_async_copy(pair, dst, sem)
        copy.start()
        return copy
    first, second = (pltpu.make_async_copy(p, dst, sem) for p in pair)

    @pl.when(flags[0] == 1)
    def _():
        first.start()

    @pl.when(flags[0] != 1)
    def _():
        second.start()

    return first


def pair_terms(scal, z_m, lo, hi, zo, acc, stats):
    a = scal[0] * LOG2E
    b = scal[1] * LOG2E

    def sims(i):
        return lax.dot_general(z_m[i:i + STEP, :], zo, (((1,), (1,)), ((), ())), preferred_element_type=F32)

    s = sims(lo)
    for i in range(lo, hi, STEP):
        ahead = sims(i + STEP) if i + STEP < hi else None
        t = jnp.exp2(s * a + b)
        d = 1.0 + t
        sig = t * pltpu.reciprocal(d, approx=False)
        q = STEP // 4
        d4 = (d[:q] * d[q:2 * q]) * (d[2 * q:3 * q] * d[3 * q:])
        stats[0] += fold(jnp.log(d4))
        stats[1] += fold(sig)
        stats[2] += fold(sig * s)
        acc[i:i + STEP, :] += jnp.dot(sig.astype(BF16), zo, preferred_element_type=F32)
        s = ahead


def first_kernel(flags, scal, w0, w1, w2, w3, m_h, m_a, o0_h, o0_a, o1_h, o1_a,
                 w_m, w_o, z_m, zf, r_out, acc, z_o, stats, w_in, f_in, sems):
    rows = f_in.shape[0] // 3
    part = w0.shape[0] // 2
    m = flags[1]
    copies = [fetch(flags, w, w_in.at[j], sems.at[j]) for j, w in enumerate((w0, w1, w2, w3))]
    copies += [
        fetch(flags, p, f_in.at[pl.ds(k * rows, rows), :], sems.at[4 + k])
        for k, p in enumerate(((m_h, m_a), (o0_h, o0_a), (o1_h, o1_a)))
    ]
    acc[...] = jnp.zeros_like(acc)
    stats[...] = jnp.zeros_like(stats)
    for j in range(4):
        copies[j].wait()
        at = pl.multiple_of((m ^ j) * part, part)
        w_m[pl.ds(at, part), :] = w_in[j, :part, :]
        w_o[pl.ds(at, part), :] = w_in[j, part:, :]
    copies[4].wait()
    zf_m, r = project(f_in[:rows, :], w_m[...])
    zf[...] = zf_m
    r_out[...] = jnp.broadcast_to(r, r_out.shape)
    z_m[...] = zf_m.astype(BF16)
    for k in range(2):
        copies[5 + k].wait()
        z_o[k * rows:(k + 1) * rows, :] = project(f_in[(k + 1) * rows:(k + 2) * rows, :], w_o[...])[0].astype(BF16)
    pair_terms(scal, z_m, 0, rows, z_o[...], acc, stats)


def embed_kernel(flags, w_o, o0, o1_h, o1_a, z_o, f_in, sems):
    rows = f_in.shape[0] // 2
    copies = [fetch(flags, p, f_in.at[pl.ds(k * rows, rows), :], sems.at[k]) for k, p in enumerate((o0, (o1_h, o1_a)))]
    for k in range(2):
        copies[k].wait()
        z_o[k * rows:(k + 1) * rows, :] = project(f_in[k * rows:(k + 1) * rows, :], w_o[...])[0].astype(BF16)


def next_kernel(flags, scal, z_m, acc_in, stats_in, own, sibling, acc, stats, z_in, z_o, sems):
    rows = z_in.shape[0]
    copies = [
        fetch(flags, z_m, z_in, sems.at[0]),
        fetch(flags, own, z_o.at[pl.ds(0, 2 * rows), :], sems.at[1]),
        fetch(flags, sibling, z_o.at[pl.ds(2 * rows, 2 * rows), :], sems.at[2]),
        fetch(flags, acc_in, acc, sems.at[3]),
        fetch(flags, stats_in, stats, sems.at[4]),
    ]
    for c in copies:
        c.wait()
    pair_terms(scal, z_in, 0, rows, z_o[...], acc, stats)


def late_kernel(flags, scal, w_m, stats_in, zo_a, zo_b, m1_h, m1_a, z_m, zf, r_out, acc, stats, f_in, z_o, sems):
    rows = f_in.shape[0]
    copies = [
        fetch(flags, (m1_h, m1_a), f_in, sems.at[0]),
        fetch(flags, stats_in, stats, sems.at[1]),
    ]
    copies += [fetch(flags, v, z_o.at[pl.ds(2 * k * rows, 2 * rows), :], sems.at[2 + k]) for k, v in enumerate((zo_a, zo_b))]
    acc[...] = jnp.zeros_like(acc)
    copies[0].wait()
    zf_m, r = project(f_in[...], w_m[...])
    zf[...] = zf_m
    r_out[...] = jnp.broadcast_to(r, r_out.shape)
    z_m[...] = zf_m.astype(BF16)
    for c in copies[1:]:
        c.wait()
    pair_terms(scal, z_m, 0, rows, z_o[...], acc, stats)


def rest_kernel(flags, scal, z_m, acc_in, stats_in, others, acc, stats, sems):
    copies = [fetch(flags, acc_in, acc, sems.at[0]), fetch(flags, stats_in, stats, sems.at[1])]
    for c in copies:
        c.wait()
    pair_terms(scal, z_m, 0, z_m.shape[0], others[...], acc, stats)


def last_kernel(width, flags, scal, z_0, z_1, zf_0, zf_1, r_0, r_1, acc_0, acc_1, stats_in, zo_a, zo_b,
                m0_h, m0_a, m1_h, m1_a, o_h, o_a,
                g_send, g_0, g_1, g_2, g_3, tail, feat, z, zf, r, z_o, z_own, acc, stats, grad, sems):
    rows = r.shape[0] // 2
    home, m, side = flags[0], flags[1], flags[2]
    scale, bias = scal[0], scal[1]

    def span(k):
        return pl.ds(k * rows, rows)

    def get(k, src, dst):
        return fetch(flags, src, dst, sems.at[k])

    now = [get(k, v, z.at[span(k), :]) for k, v in enumerate((z_0, z_1))]
    now += [get(2, (o_h, o_a), z_o), get(3, stats_in, stats)]
    now += [get(4 + k, v, acc.at[span(k), :]) for k, v in enumerate((acc_0, acc_1))]
    rest = [get(6 + k, v, zf.at[span(k), :]) for k, v in enumerate((zf_0, zf_1))]
    rest += [get(8 + k, v, r.at[span(k), :]) for k, v in enumerate((r_0, r_1))]
    rest += [get(10 + k, v, feat.at[span(k), :]) for k, v in enumerate(((m0_h, m0_a), (m1_h, m1_a)))]
    first = (zo_a.at[span(0), :], zo_b.at[span(1), :])
    second = (zo_a.at[span(1), :], zo_b.at[span(0), :])
    rest += [get(12 + k, v, z_own.at[span(k), :]) for k, v in enumerate((first, second))]
    for c in now:
        c.wait()
    pair_terms(scal, z, 0, 2 * rows, z_o[...], acc, stats)
    for c in rest:
        c.wait()

    def finish(k):
        at = slice(k * rows, (k + 1) * rows)
        pair = z_own[at, :].astype(F32)
        s = jnp.sum(z[at, :].astype(F32) * pair, axis=1, keepdims=True)
        l = scale * s + bias
        t = jnp.exp2(s * (scale * LOG2E) + bias * LOG2E)
        rest = pltpu.reciprocal(1.0 + t, approx=False)
        change = (-rest).astype(BF16).astype(F32) - (t * rest).astype(BF16).astype(F32)
        dz = (scale / width) * (acc[at, :] + change * pair)
        zf_k = zf[at, :]
        du = (r[at, :1] * (dz - zf_k * jnp.sum(zf_k * dz, axis=1, keepdims=True))).astype(BF16)
        return du, jnp.sum(s), jnp.sum(l)

    def gradient(k, du):
        return lax.dot_general(feat[k * rows:(k + 1) * rows, :], du, (((0,), (0,)), ((), ())), preferred_element_type=F32)

    du_0, s_0, l_0 = finish(0)
    part_0 = gradient(0, du_0)
    du_1, s_1, l_1 = finish(1)
    grad[...] = part_0 + gradient(1, du_1)
    half = grad.shape[0] // 8

    def piece(j, h):
        return grad[pl.ds(pl.multiple_of((m ^ j) * 2 * half + (side ^ h) * half, half), half), :]

    for k, (j, h) in enumerate(((0, 0), (0, 1), (2, 0), (2, 1))):
        g_send[k * half:(k + 1) * half, :] = piece(j ^ 1, h)
        (g_0, g_1, g_2, g_3)[k][...] = piece(j, h)
    most = jnp.max(jnp.abs(grad[...]))
    loss = (jnp.sum(stats[0]) - (l_0 + l_1)) / width
    gsum = (jnp.sum(stats[1]) - 2 * rows) / width
    gscale = scale * (jnp.sum(stats[2]) - (s_0 + s_1)) / width
    row = lax.broadcasted_iota(jnp.int32, tail.shape, 0)
    values = jnp.zeros(tail.shape, F32)
    for k, v in enumerate((most, loss, gsum, gscale)):
        values = jnp.where(row == k, v, values)
    tail[...] = values
    g_send[4 * half:, :] = values


def call(kernel, outs, inputs, scratch, sems, resident=(), limit=32):
    def spec(k, v):
        return SMEM if v.ndim == 1 else VMEM if k in resident else ANY

    return pl.pallas_call(
        kernel,
        out_shape=[jax.ShapeDtypeStruct(*o) for o in outs],
        in_specs=[spec(k, v) for k, v in enumerate(inputs)],
        out_specs=[VMEM] * len(outs),
        scratch_shapes=[pltpu.VMEM(*s) for s in scratch] + [pltpu.SemaphoreType.DMA((sems,))],
        compiler_params=pltpu.CompilerParams(vmem_limit_bytes=limit * 2**20),
        cost_estimate=pl.CostEstimate(flops=1, bytes_accessed=1, transcendentals=0),
    )(*inputs)


def encode(values, tail):
    return (values * (16384.0 / (tail[:1] + 1e-30))).astype(F16)


def decode(message, tail):
    return message.astype(F32) * ((tail[:1] + 1e-30) * (1.0 / 16384.0))


def top_row(v):
    return lax.broadcasted_iota(jnp.int32, v.shape, 0) == 0


def encode_with_tail(values, tail):
    power = jnp.ceil(jnp.log2(tail[:1] + 1e-30))
    tail = jnp.where(top_row(tail), power, tail * (1.0 / 64.0))
    high = lax.reduce_precision(tail, exponent_bits=5, mantissa_bits=10)
    return jnp.concatenate([values * jnp.exp2(14.0 - power), high, tail - high], axis=0).astype(F16)


def decode_tail(message):
    rows = message.shape[0] - 16
    tail = message[rows:rows + 8].astype(F32) + message[rows + 8:].astype(F32)
    return jnp.where(top_row(tail), jnp.exp2(tail), tail * 64.0)


def decode_with_tail(message):
    rows = message.shape[0] - 16
    power = message[rows:rows + 1].astype(F32)
    return message[:rows].astype(F32) * jnp.exp2(power - 14.0), decode_tail(message)


def per_device(n_batch, img_feat, txt_feat, img_proj, txt_proj, logit_scale, bias):
    rows, wide = img_feat.shape
    embed = img_proj.shape[1]
    n = n_batch * 4
    width = 8 * rows
    b = lax.axis_index("batch")
    m = lax.axis_index("mp")
    role, side, zh, c = b & 1, b >> 1 & 1, b >> 2 & 1, m & 1
    home = (c == zh).astype(jnp.int32)
    images = role == 0
    flags = jnp.stack([home, m, side])
    scal = jnp.stack([jnp.exp(logit_scale), bias])

    def send(v, home, away, name):
        with jax.named_scope(name):
            return lax.ppermute(v, AXES, pairs(n, home, away))

    def both(v, flip, name):
        return send(v, flip, flip, name)

    swap = ZH | C
    mine = jnp.where(images, img_feat, txt_feat)
    opp = jnp.where(images, txt_feat, img_feat)
    w0 = jnp.concatenate([jnp.where(images, img_proj, txt_proj), jnp.where(images, txt_proj, img_proj)], axis=0)
    p1 = send(mine, ROLE, swap, "mine_swap")
    w2 = both(w0, X, "proj_x")
    w1 = both(w0, C, "proj_core")
    s0 = send(opp, C, None, "sib_opp")
    p0 = send(opp, SIDE, None, "opp_home_side")
    w3 = both(w2, C, "proj_xcore")
    w2, p0 = lax.optimization_barrier((w2, p0))
    p1, w2, opp_late = lax.optimization_barrier((p1, w2, opp))
    p2 = send(opp_late, ROLE, swap, "opp_swap")
    p3 = send(p1, SIDE, ROLE, "mine_square")
    s1 = send(p1, C, None, "sib_mine")

    square = (wide, embed)
    one, two = (rows, embed), (2 * rows, embed)
    norm = (rows, 128)
    stat = (3, 8, LANES)
    w_m, w_o, z_0, zf_0, r_0, acc_0, zo_a, stats = call(
        first_kernel,
        [(square, BF16), (square, BF16), (one, BF16), (one, F32), (norm, F32), (one, F32), (two, BF16), (stat, F32)],
        [flags, scal, w0, w1, w2, w3, mine, p1, opp, s0, p1, s1],
        [((4, *w0.shape), BF16), ((3 * rows, wide), BF16)],
        7,
    )
    p2, p3, w_o = lax.optimization_barrier((p2, p3, w_o))
    p6 = send(p2, None, ROLE, "opp_square_role")
    (zo_b,) = call(embed_kernel, [(two, BF16)], [flags, w_o, p3, p0, p2], [(two, BF16)], 2, (1,))
    zo_c = both(zo_b, C, "sib_square")
    p4 = send(zo_b, None, SIDE, "square_side")
    acc_0, stats = call(
        next_kernel,
        [(one, F32), (stat, F32)],
        [flags, scal, z_0, acc_0, stats, zo_b, zo_c],
        [(one, BF16), ((4 * rows, embed), BF16)],
        5,
    )
    p6, acc_0, stats = lax.optimization_barrier((p6, acc_0, stats))
    z_1, zf_1, r_1, acc_1, stats = call(
        late_kernel,
        [(one, BF16), (one, F32), (norm, F32), (one, F32), (stat, F32)],
        [flags, scal, w_m, stats, zo_a, zo_b, p2, p6],
        [(one, BF16), ((4 * rows, embed), BF16)],
        4,
        (2,),
    )
    p4, acc_1 = lax.optimization_barrier((p4, acc_1))
    s4 = send(p4, None, C, "sib_side")
    acc_1, stats = call(
        rest_kernel,
        [(one, F32), (stat, F32)],
        [flags, scal, z_1, acc_1, stats, zo_c],
        [],
        2,
        (2, 5),
    )
    half = wide // 8
    pieces, *kept, tail = call(
        functools.partial(last_kernel, width),
        [((4 * half + 8, embed), F32)] + [((half, embed), F32)] * 4 + [((8, embed), F32)],
        [flags, scal, z_0, z_1, zf_0, zf_1, r_0, r_1, acc_0, acc_1, stats, zo_a, zo_b, mine, p1, p2, p6, s4, p4],
        [
            (two, BF16), (two, BF16), (two, F32), ((2 * rows, 128), F32), (two, BF16), (two, BF16), (two, F32),
            (stat, F32), (square, F32),
        ],
        14,
    )

    got = both(pieces, C, "core_sum")
    tail = tail + got[4 * half:]
    kept = [v + got[k * half:(k + 1) * half] for k, v in enumerate(kept)]
    messages = lax.optimization_barrier(tuple(encode_with_tail(v, tail) for v in kept[1:]))
    ways = (SIDE, X, X | SIDE)
    came = lax.optimization_barrier(tuple(both(v, flip, "square_sum") for v, flip in zip(messages, ways)))
    parts = [decode_with_tail(v) for v in came]
    tails = [decode_tail(messages[0])] + [t for _, t in parts]
    total = (kept[0] + parts[0][0]) + (parts[1][0] + parts[2][0])
    tail = (tails[0] + tails[1]) + (tails[2] + tails[3])
    flip = ZH
    while flip < n:
        message, tail = lax.optimization_barrier((encode(total, tail), tail))
        other, more = lax.optimization_barrier((both(message, flip, "half_sum"), both(tail, flip, "half_sum")))
        total = decode(message, tail) + decode(other, more)
        tail = tail + more
        flip *= 2
    message, tail = lax.optimization_barrier((encode(total, tail), tail))
    by_s, by_r, by_rs, more = lax.optimization_barrier((
        both(message, SIDE, "hand_out"),
        both(message, ROLE, "hand_out"),
        both(message, ROLE | SIDE, "hand_out"),
        both(tail, ROLE, "hand_out"),
    ))

    def order(first, second, t):
        first, second = decode(first, t), decode(second, t)
        return jnp.concatenate([jnp.where(side == 0, first, second), jnp.where(side == 0, second, first)], axis=0)

    here, there = order(message, by_s, tail), order(by_r, by_rs, more)
    sums = jnp.where(images, tail, more)[:, 0] / (rows * n)
    return (sums[1], sums[3], sums[2], jnp.where(images, here, there), jnp.where(images, there, here))


def solution(mesh):
    return jax.shard_map(
        functools.partial(per_device, mesh.shape["batch"]),
        mesh=mesh,
        in_specs=(
            P(AXES, None),
            P(AXES, None),
            P("mp", None),
            P("mp", None),
            P(),
            P(),
        ),
        out_specs=(P(), P(), P(), P("mp", None), P("mp", None)),
        check_vma=False,
    )
```
